128 devices in a mesh: slab: 32 (over x, y_hi, z), sub: 4 (over y_lo, core).
Axes of the slice: x: 4, y: 4 (y_hi: 2, y_lo: 2; y = y_hi * 2 + y_lo), z: 4, core: 2. Of those that a mesh axis runs over, the one named last changes fastest.
Arguments:
- mm_atoms: float32 [4, 2097152], P(None, ('slab', 'sub')), may hold values from -6 to 6
- neighbours: int32 [16, 2097152], P(None, ('slab', 'sub')), may hold values from 0 to 18431, as said below
- embed_blocks: int32 [128, 8], P(('slab', 'sub')), may hold values from 0 to 127, as said below
- embed_count: int32 [128], P(('slab', 'sub')), may hold values from 1 to 8
- ml_coords: float32 [3, 5120], P(None, ('slab', 'sub')), may hold values from -6 to 6
- ml_species: int32 [5120], P(('slab', 'sub')), may hold values from 0 to 9
- ml_edges: int32 [5120, 32], P(('slab', 'sub')), may hold values from 0 to 5119
- species_table: float32 [10, 256], replicated, may hold values from -6 to 6
- field_weight: float32 [256], replicated, may hold values from -4 to 4
- msg_weight: bfloat16 [2, 256, 256], replicated, may hold values from -0.375 to 0.375
- radial_weight: float32 [2, 8, 256], replicated, may hold values from -6 to 6
- mix_weight: bfloat16 [2, 256, 256], replicated, may hold values from -0.375 to 0.375
- charge_weight: float32 [256], replicated, may hold values from -0.375 to 0.375
- energy_weight: float32 [256], replicated, may hold values from -0.375 to 0.375
Outputs:
- ml_energy: float32 [5120], P(('slab', 'sub'))
- mm_force: float32 [3, 2097152], P(None, ('slab', 'sub'))
The draws below stay inside these ranges and needn't reach their ends.
Inputs may be any that keep to these rules, and one draw needn't show every extreme that they name: `neighbours`: slot p of 2097152 atom a on any device holds 1024 + a + o with -1024 <= o <= 1024; o = 0 marks an empty slot (an atom paired with itself). `embed_blocks`: the blocks listed for one device are distinct.
All inputs are finite; a program needn't handle non-finite values.
Results may differ from the reference program's by a relative error of at most 0.00055.
Values may be sent and summed in bfloat16 or wider, within the bound.
No kernel may reach another device: no remote copies, remote signals or barrier semaphores. Data moves between devices by JAX's collectives and lax.ppermute only.
A program may use at most 320 MiB of HBM per device.

```python
import jax
import jax.numpy as jnp
from jax import lax

C = 256
NRAD = 8
NSPEC = 10
LAYERS = 2
KNB = 32
PPA = 16
EMB_MAX = 8
ML_DEV = 40
MM_DEV = 16384
NDEV = 128
ML = 5120
MM = 2097152
HALO = 1024
NBLK = 128
EMB = 1024


def draw_neighbours(key, part):
    key = jax.random.fold_in(key, 11)
    offsets = jax.random.randint(key, (PPA, NDEV, MM_DEV), -HALO, HALO + 1)
    atom_ids = jnp.arange(MM_DEV, dtype=jnp.int32)
    slot_ids = jnp.arange(PPA, dtype=jnp.int32)[:, None, None]
    empty_slot = (slot_ids == PPA - 1) & (atom_ids[None, None, :] % 4 == 0)
    offsets = jnp.where(empty_slot, 0, offsets)
    offsets = offsets.at[0, :, 0].set(-HALO)
    offsets = offsets.at[0, :, MM_DEV - 1].set(HALO)
    listed = HALO + atom_ids[None, None, :] + offsets
    return listed.reshape(PPA, NDEV * MM_DEV).astype(jnp.int32)


def draw_embed_blocks(key, part):
    key = jax.random.fold_in(key, 12)
    dev_keys = jax.random.split(key, NDEV)
    picked = jax.vmap(lambda one_key: jax.random.permutation(one_key, NBLK)[:EMB_MAX])(dev_keys)
    return picked.astype(jnp.int32)


def draw_embed_count(key, part):
    key = jax.random.fold_in(key, 13)
    centre = jax.random.randint(key, (), 0, NDEV)
    dev_ids = jnp.arange(NDEV, dtype=jnp.int32)
    spread = max(NDEV // (2 * EMB_MAX), 1)
    distance = jnp.abs(dev_ids - centre) // spread
    return jnp.maximum(EMB_MAX - distance, 1).astype(jnp.int32)


def with_ends(values, key, low, top_value):
    spot = [jax.random.randint(jax.random.fold_in(key, axis), (), 0, length) for axis, length in enumerate(values.shape)]
    longest = values.shape.index(max(values.shape))
    beside = spot[:longest] + [(spot[longest] + 1) % values.shape[longest]] + spot[longest + 1:]
    return values.at[tuple(spot)].set(low).at[tuple(beside)].set(top_value)


def shard_levels(own_key, dims, cuts, low, top_value):
    level, own = 1.0, jax.random.fold_in(own_key, 6)
    for dim, parts in cuts:
        heights = jnp.exp(jax.random.uniform(jax.random.fold_in(own, dim), (parts,), jnp.float32, low / len(cuts), top_value / len(cuts)))
        level = level * jnp.repeat(heights, dims[dim] // parts).reshape([-1 if axis == dim else 1 for axis in range(len(dims))])
    return level


def bell_draw(key, shape, scale, bound, shards=(), held_as=jnp.bfloat16):
    values = scale * jax.random.normal(key, shape, jnp.float32)
    if shards:
        values = values * shard_levels(key, shape, shards, -0.22, 0.18)
    return jnp.clip(values, -bound, bound).astype(held_as)


def setup_inputs(seed: int = 0) -> dict:
    streams_of = jax.random.split(jax.random.key(seed), 15)
    return {
        "mm_atoms": bell_draw(streams_of[0], (4, MM), 1.0, 6.0, ((1, 128),), jnp.float32),
        "neighbours": draw_neighbours(jax.random.fold_in(streams_of[14], 71), 0),
        "embed_blocks": draw_embed_blocks(jax.random.fold_in(streams_of[14], 71), 0),
        "embed_count": draw_embed_count(jax.random.fold_in(streams_of[14], 71), 0),
        "ml_coords": bell_draw(streams_of[4], (3, ML), 1.0, 6.0, ((1, 128),), jnp.float32),
        "ml_species": with_ends(jax.random.randint(streams_of[5], (ML,), 0, NSPEC), jax.random.fold_in(streams_of[5], 1), 0, NSPEC - 1).astype(jnp.int32),
        "ml_edges": with_ends(jax.random.randint(streams_of[6], (ML, KNB), 0, ML), jax.random.fold_in(streams_of[6], 1), 0, ML - 1).astype(jnp.int32),
        "species_table": bell_draw(streams_of[7], (NSPEC, C), 1.0, 6.0, (), jnp.float32),
        "field_weight": bell_draw(streams_of[8], (C,), 0.3, 4.0, (), jnp.float32),
        "msg_weight": bell_draw(streams_of[9], (LAYERS, C, C), C ** -0.5, 0.375),
        "radial_weight": bell_draw(streams_of[10], (LAYERS, NRAD, C), 0.5, 6.0, (), jnp.float32),
        "mix_weight": bell_draw(streams_of[11], (LAYERS, C, C), C ** -0.5, 0.375),
        "charge_weight": bell_draw(streams_of[12], (C,), C ** -0.5, 0.375, (), jnp.float32),
        "energy_weight": bell_draw(streams_of[13], (C,), C ** -0.5, 0.375, (), jnp.float32),
    }


radial_gamma = 2.0
radial_step = 0.5

def reference(mm_atoms, neighbours, embed_blocks, embed_count, ml_coords, ml_species, ml_edges, species_table, field_weight, msg_weight, radial_weight, mix_weight, charge_weight, energy_weight):
    dev_ids = jnp.arange(NDEV, dtype=jnp.int32)
    local_nb = neighbours.reshape(PPA, NDEV, MM_DEV).transpose(1, 0, 2)
    atoms_dev = mm_atoms.reshape(4, NDEV, MM_DEV).transpose(1, 0, 2)

    def pair_block(inputs):
        dev, nb_block, centre = inputs
        global_ids = (dev * MM_DEV + nb_block - HALO) % MM
        partner = mm_atoms[:, global_ids]
        offset_vec = centre[:3, None, :] - partner[:3]
        dist_sq = lax.optimization_barrier(jnp.sum(offset_vec * offset_vec, axis=0)) + 1.0
        strength = centre[3][None, :] * partner[3] * dist_sq ** (-1.5)
        return lax.optimization_barrier(jnp.sum(strength[None] * offset_vec, axis=1))
    pair_force = lax.map(pair_block, (dev_ids, local_nb, atoms_dev))
    pair_force = pair_force.transpose(1, 0, 2).reshape(3, MM)
    slot_ids = (dev_ids[:, None, None] * MM_DEV + embed_blocks[:, :, None] * 128 + jnp.arange(128, dtype=jnp.int32)[None, None, :]).reshape(-1)
    live_slot = (jnp.arange(EMB_MAX, dtype=jnp.int32)[None, :] < embed_count[:, None]).astype(jnp.float32)
    live_slot = jnp.broadcast_to(live_slot[:, :, None], (NDEV, EMB_MAX, 128)).reshape(-1)
    embed_atoms = mm_atoms[:, slot_ids]
    embed_atoms = jnp.concatenate([embed_atoms[:3], (embed_atoms[3] * live_slot)[None]], axis=0)
    coupling = 4.0 / jnp.sqrt(jnp.float32(ML))
    field_coupling = 3.0 / jnp.sqrt(jnp.float32(NDEV * EMB))

    def field_block(coords):
        dist_sq = jnp.zeros((coords.shape[1], embed_atoms.shape[1]), jnp.float32)
        for coord in range(3):
            gap = coords[coord][:, None] - embed_atoms[coord][None, :]
            dist_sq = dist_sq + gap * gap
        return field_coupling * lax.optimization_barrier(jnp.sum(embed_atoms[3][None, :] * lax.rsqrt(dist_sq + 1.0), axis=1))
    potential = lax.map(field_block, ml_coords.reshape(3, NDEV, ML_DEV).transpose(1, 0, 2)).reshape(ML)
    features = species_table[ml_species] + potential[:, None] * field_weight[None, :]
    partner_pos = ml_coords[:, ml_edges]
    gaps = ml_coords[:, :, None] - partner_pos
    distance = jnp.sqrt(lax.optimization_barrier(jnp.sum(gaps * gaps, axis=0)))
    basis_mu = radial_step * jnp.arange(NRAD, dtype=jnp.float32)
    radial_basis = jnp.exp(-radial_gamma * (distance[..., None] - basis_mu) ** 2)
    for layer_idx in range(LAYERS):
        projected = jnp.dot(features.astype(jnp.bfloat16), msg_weight[layer_idx], preferred_element_type=jnp.float32).astype(jnp.bfloat16)
        radial = jnp.einsum('ikb,bc->ikc', radial_basis, radial_weight[layer_idx], precision=lax.Precision.HIGHEST)
        message = lax.optimization_barrier(jnp.mean(radial * projected[ml_edges].astype(jnp.float32), axis=1)).astype(jnp.bfloat16)
        features = features + jax.nn.silu(jnp.dot(message, mix_weight[layer_idx], preferred_element_type=jnp.float32))
    charge = jnp.tanh(jnp.dot(features, charge_weight, precision=lax.Precision.HIGHEST))
    ml_energy = jnp.dot(features, energy_weight, precision=lax.Precision.HIGHEST) + charge * potential

    def force_block(slots):
        dist_sq = jnp.zeros((ML, slots.shape[1]), jnp.float32)
        gaps_list = []
        for coord in range(3):
            gap = slots[coord][None, :] - ml_coords[coord][:, None]
            gaps_list.append(gap)
            dist_sq = dist_sq + gap * gap
        inv_cube = (dist_sq + 1.0) ** (-1.5)
        weighted = charge[:, None] * inv_cube
        return jnp.stack([coupling * slots[3] * lax.optimization_barrier(jnp.sum(weighted * gap, axis=0)) for gap in gaps_list])
    embed_force = lax.map(force_block, embed_atoms.reshape(4, NDEV, EMB).transpose(1, 0, 2))
    embed_force = embed_force.transpose(1, 0, 2).reshape(3, NDEV * EMB)
    mm_force = pair_force.at[:, slot_ids].add(embed_force)
    return (ml_energy, mm_force)
```

```python
import functools
import math

import jax
import jax.numpy as jnp
from jax import lax
from jax.experimental import pallas as pl
from jax.experimental.pallas import tpu as pltpu
from jax.sharding import Mesh
from jax.sharding import PartitionSpec as P

ALL = ("x", "yh", "z", "yl", "c")
Y = ("yh", "yl")
vmem_mib = lambda size: pltpu.CompilerParams(vmem_limit_bytes=size * 1024 * 1024)
LANES = 128
NDEV = 128
ML_DEV = 40
KNB = 32
EDGES = ML_DEV * KNB
ROWS = 1344
HALO_BLOCKS = 8
PAIR_STEP = 4


def rows0(left, right):
    return lax.dot_general(
        left, right, (((0,), (0,)), ((), ())), preferred_element_type=jnp.float32
    )


def pair_kernel(first, count, left, own, right, nb, after, out, zero, ext):
    own_blocks = own.shape[1] // LANES
    step = pl.program_id(0)

    @pl.when(step == 0)
    def _():
        zero[...] = jnp.zeros_like(zero)
        low, high = first - HALO_BLOCKS, first + count + HALO_BLOCKS
        for src, begin, size in ((left, -HALO_BLOCKS, HALO_BLOCKS), (own, 0, own_blocks), (right, own_blocks, HALO_BLOCKS)):
            start, stop = max(low, begin), min(high, begin + size)
            if start >= stop:
                continue

            def fill(r, carry, src=src, begin=begin):
                rows = src[:, pl.ds(pl.multiple_of((r - begin) * LANES, LANES), LANES)]
                for c in range(4):
                    ext[c, r - low] = jnp.broadcast_to(rows[c : c + 1], (8, LANES))
                return carry

            lax.fori_loop(start, stop, fill, 0)

    blocks = nb.shape[1] // LANES

    def block(j, carry):
        b = step * blocks + j
        lanes = pl.ds(pl.multiple_of(j * LANES, LANES), LANES)
        rel = nb[:, lanes] - (b + first) * LANES
        row = rel >> 7
        lane = rel & 127
        centre = [ext[c, b + HALO_BLOCKS] for c in range(4)]
        total = [jnp.zeros((8, LANES), jnp.float32) for _ in range(3)]
        for h in range(nb.shape[0] // 8):
            near = row[8 * h : 8 * h + 8]
            pick = lane[8 * h : 8 * h + 8]
            got = [jnp.zeros((8, LANES), jnp.float32) for _ in range(4)]
            for k in range(2 * HALO_BLOCKS + 1):
                here = near == k
                for c in range(4):
                    value = jnp.take_along_axis(ext[c, b + k], pick, axis=1, mode="promise_in_bounds")
                    got[c] = jnp.where(here, value, got[c])
            off = [centre[c] - got[c] for c in range(3)]
            inv = lax.rsqrt(off[0] * off[0] + off[1] * off[1] + off[2] * off[2] + 1.0)
            strength = centre[3] * got[3] * (inv * inv * inv)
            for c in range(3):
                total[c] = total[c] + strength * off[c]
        for c in range(3):
            out[c : c + 1, lanes] = jnp.sum(total[c], axis=0, keepdims=True)
        return carry

    lax.fori_loop(0, blocks, block, 0, unroll=PAIR_STEP)


def pair_forces(first, count, left, own, right, neighbours, after):
    wide = PAIR_STEP * LANES
    whole = lambda a: pl.BlockSpec(a.shape, lambda i: (0, 0))
    slots = neighbours.shape[0]
    return pl.pallas_call(
        functools.partial(pair_kernel, first, count),
        grid=(count // PAIR_STEP,),
        out_shape=(
            jax.ShapeDtypeStruct((3, count * LANES), jnp.float32),
            jax.ShapeDtypeStruct((1, HALO_BLOCKS * LANES), jnp.float32),
        ),
        in_specs=[
            whole(left),
            whole(own),
            whole(right),
            pl.BlockSpec((slots, wide), lambda i: (0, i + first // PAIR_STEP)),
            pl.BlockSpec(memory_space=pl.ANY),
        ],
        out_specs=(
            pl.BlockSpec((3, wide), lambda i: (0, i)),
            pl.BlockSpec((1, HALO_BLOCKS * LANES), lambda i: (0, 0)),
        ),
        scratch_shapes=[pltpu.VMEM((4, count + 2 * HALO_BLOCKS, 8, LANES), jnp.float32)],
        compiler_params=vmem_mib(6),
        cost_estimate=pl.CostEstimate(
            flops=count * 10**7, bytes_accessed=count * 16384, transcendentals=count * slots * LANES
        ),
        name="pair_forces",
    )(left, own, right, neighbours, after)


def spread_kernel(coords, species, out):
    rows = [coords[c : c + 1, :] for c in range(3)] + [species[...].astype(jnp.float32)]
    rows = rows[:3] + [jnp.zeros((1, 8), jnp.float32)] + rows[3:] + [jnp.zeros((1, LANES - ML_DEV), jnp.float32)]
    out[:, 0, :] = jnp.broadcast_to(jnp.concatenate(rows, axis=1), (NDEV, 2 * LANES))


def spread(coords, species):
    vmem = pl.BlockSpec(memory_space=pltpu.VMEM)
    return pl.pallas_call(
        spread_kernel,
        out_shape=jax.ShapeDtypeStruct((NDEV, 1, 2 * LANES), jnp.float32),
        in_specs=[vmem, vmem],
        out_specs=vmem,
        name="spread",
    )(coords, species)


def three_parts(value):
    one = value.astype(jnp.bfloat16).astype(jnp.float32)
    rest = value - one
    two = rest.astype(jnp.bfloat16).astype(jnp.float32)
    three = (rest - two).astype(jnp.bfloat16).astype(jnp.float32)
    return one, two, three


def field_kernel(scale, blocks, count, mm, tab, after, pot, atoms, slots, p8, qb):
    turned = tab[:, :LANES].T
    x, y, z = (turned[ML_DEV * c : ML_DEV * (c + 1)] for c in range(3))
    p8[...] = jnp.zeros_like(p8)
    for c, value in enumerate((x, y, z, x * x + y * y + z * z, jnp.ones_like(x))):
        p8[pl.ds(c, ML_DEV, stride=8), :] = value

    def atom_tile(t, carry):
        one, two, three = three_parts(p8[pl.ds(pl.multiple_of(t * 8, 8), 8), :])
        atoms[:, pl.ds(pl.multiple_of(t * LANES, LANES), LANES)] = jnp.concatenate(
            [one, one, two, two, one, three], axis=0
        ).astype(jnp.bfloat16)
        return carry

    lax.fori_loop(0, ML_DEV, atom_tile, 0)
    nslots = blocks.shape[1]
    for s in range(nslots):
        rows = mm[:, pl.ds(pl.multiple_of(blocks[0, s] * LANES, LANES), LANES)]
        q = rows[3:4] * jnp.where(s < count[0], 1.0, 0.0)
        pos = rows[:3]
        norm = jnp.sum(pos * pos, axis=0, keepdims=True) + 1.0
        eight = jnp.concatenate(
            [-2.0 * pos, jnp.ones_like(q), norm, jnp.zeros((3, LANES), jnp.float32)], axis=0
        )
        one, two, three = three_parts(eight)
        slots[:, s * LANES : (s + 1) * LANES] = jnp.concatenate(
            [one, two, one, two, three, one], axis=0
        ).astype(jnp.bfloat16)
        qb[s * LANES : (s + 1) * LANES, :] = jnp.broadcast_to(q, (LANES, LANES)).T

    def tile(i, carry):
        right = atoms[:, pl.ds(pl.multiple_of(i * 256, 256), 256)]
        total = jnp.zeros((8, 256), jnp.float32)
        for s in range(nslots // 2):
            inv = lax.rsqrt(rows0(slots[:, s * 256 : (s + 1) * 256], right))
            q = qb[s * 256 : (s + 1) * 256, :]
            term = inv * jnp.concatenate([q, q], axis=1)
            total = total + jnp.sum(term.reshape(32, 8, 256), axis=0)
        total = scale * jnp.sum(total, axis=0, keepdims=True)
        pot[pl.ds(2 * i, 1), :] = total[:, :LANES]
        pot[pl.ds(2 * i + 1, 1), :] = total[:, LANES:]
        return carry

    lax.fori_loop(0, ML_DEV // 2, tile, 0, unroll=5)


def field(blocks, count, mm, tab, after, scale):
    nslots = blocks.shape[1]
    smem = pl.BlockSpec(memory_space=pltpu.SMEM)
    vmem = pl.BlockSpec(memory_space=pltpu.VMEM)
    return pl.pallas_call(
        functools.partial(field_kernel, scale),
        out_shape=(
            jax.ShapeDtypeStruct((ML_DEV, LANES), jnp.float32),
            pltpu.HBM((48, ML_DEV * LANES), jnp.bfloat16),
            pltpu.HBM((48, nslots * LANES), jnp.bfloat16),
        ),
        in_specs=[smem, smem, vmem, vmem, pl.BlockSpec(memory_space=pl.ANY)],
        out_specs=(vmem,) * 3,
        scratch_shapes=[
            pltpu.VMEM((8 * ML_DEV, LANES), jnp.float32),
            pltpu.VMEM((nslots * LANES, LANES), jnp.float32),
        ],
        compiler_params=vmem_mib(10),
        name="field",
    )(blocks, count, mm, tab, after)


def lane_iota(shape):
    return lax.broadcasted_iota(jnp.int32, shape, 1)


def exact_pick(left, right):
    left = left.astype(jnp.bfloat16)
    parts = [jnp.dot(left, part.astype(jnp.bfloat16), preferred_element_type=jnp.float32) for part in three_parts(right)]
    return (parts[2] + parts[1]) + parts[0]


def exact_sum(left, right):
    right = right.astype(jnp.bfloat16)
    parts = [jnp.dot(part.astype(jnp.bfloat16), right, preferred_element_type=jnp.float32) for part in three_parts(left)]
    return (parts[2] + parts[1]) + parts[0]


def where_is(me, ids):
    own_ids = me * ML_DEV + jnp.minimum(lax.broadcasted_iota(jnp.int32, (ROWS - EDGES, 1), 0), ML_DEV - 1)
    atom = jnp.concatenate([ids, own_ids], axis=0)
    dev = (atom * 52429) >> 21
    return dev, atom - dev * ML_DEV


def geometry_kernel(me, ids, tab, after, basis_out, kinds_out, zero):
    zero[...] = jnp.zeros_like(zero)
    dev, t = where_is(me[0], ids[...])
    at_dev = lane_iota((ROWS, LANES)) == dev
    rows = exact_pick(jnp.where(at_dev, 1.0, 0.0), tab[...])
    lane = lane_iota((1, 2 * LANES))
    place = jnp.where(lane < ML_DEV, lane, jnp.where(lane < 2 * ML_DEV, lane - ML_DEV, lane - 2 * ML_DEV))
    place = jnp.where(lane < LANES, place, lane - LANES)
    place = jnp.where(place < ML_DEV, place, -1)
    rows = jnp.where(place == t, rows, 0.0)
    src = lax.broadcasted_iota(jnp.int32, (2 * LANES, LANES), 0)
    dst = lane_iota((2 * LANES, LANES))
    group = jnp.where(src < ML_DEV, 0, jnp.where(src < 2 * ML_DEV, 1, jnp.where(src < LANES, 2, 3)))
    picked = exact_sum(rows, jnp.where(group == dst, 1.0, 0.0))
    own = picked[EDGES : EDGES + ML_DEV]
    centre = jnp.broadcast_to(own[:, None, :], (ML_DEV, KNB, LANES)).reshape(EDGES, LANES)
    gap = picked[:EDGES] - centre
    lanes = lane_iota((EDGES, LANES))
    dist = jnp.sqrt(exact_sum(jnp.where(lanes < 3, gap * gap, 0.0), jnp.ones((LANES, LANES), jnp.float32)))
    shift = dist - 0.5 * (lanes & 7).astype(jnp.float32)
    one, two, three = three_parts(jnp.exp(-2.0 * (shift * shift)))
    part = lanes >> 3
    value = jnp.where((part < 2) | (part == 4), one, jnp.where(part < 4, two, three))
    basis_out[...] = jnp.where(part < 6, value, 0.0).astype(jnp.bfloat16)
    kind = jnp.broadcast_to(picked[:, 3:4], (ROWS, LANES)).astype(jnp.int32)
    lanes = lane_iota((ROWS, LANES))
    kinds_out[...] = jnp.where((kind == (lanes & 15)) & (lanes < 48), 1.0, 0.0).astype(jnp.bfloat16)


def geometry(me, ids, tab, after):
    smem = pl.BlockSpec(memory_space=pltpu.SMEM)
    vmem = pl.BlockSpec(memory_space=pltpu.VMEM)
    return pl.pallas_call(
        geometry_kernel,
        out_shape=(
            jax.ShapeDtypeStruct((EDGES, LANES), jnp.bfloat16),
            jax.ShapeDtypeStruct((ROWS, LANES), jnp.bfloat16),
            jax.ShapeDtypeStruct((1, LANES), jnp.float32),
        ),
        in_specs=[smem, vmem, vmem, pl.BlockSpec(memory_space=pl.ANY)],
        out_specs=(vmem,) * 3,
        compiler_params=vmem_mib(20),
        name="geometry",
    )(me, ids, tab, after)


def radial_of(basis, weights):
    one, two, three = three_parts(weights)
    rest = jnp.zeros((LANES - 48, weights.shape[1]), jnp.float32)
    stacked = jnp.concatenate([one, two, one, two, three, one, rest], axis=0).astype(jnp.bfloat16)
    return jnp.dot(basis, stacked, preferred_element_type=jnp.float32)


def first_layer_kernel(
    me, ids, pot, basis, kinds, table, field_w, msg, radial_w, mix, feat_out, proj_out
):
    pot_rows = jnp.concatenate([pot[...], jnp.zeros((LANES - ML_DEV, LANES), jnp.float32)], axis=0).T
    dev, t = where_is(me[0], ids[...])
    lanes = lane_iota((ROWS, LANES))
    rows = exact_pick(jnp.where(lanes == dev, 1.0, 0.0), pot_rows)
    pot_of = jnp.sum(jnp.where(lanes == t, rows, 0.0), axis=1, keepdims=True)
    channels = msg.shape[1]
    lines = jnp.concatenate([table[...], jnp.zeros((16 - table.shape[0], channels), jnp.float32)], axis=0)
    lines = jnp.concatenate(three_parts(lines) + (jnp.zeros((LANES - 48, channels), jnp.float32),), axis=0)
    feat = jnp.dot(kinds[...], lines.astype(jnp.bfloat16), preferred_element_type=jnp.float32)
    feat = feat + pot_of * field_w[...]
    proj = jnp.dot(feat[:EDGES].astype(jnp.bfloat16), msg[0], preferred_element_type=jnp.float32)
    proj = proj.astype(jnp.bfloat16).astype(jnp.float32)
    radial = radial_of(basis[...], radial_w[0])
    message = jnp.sum((radial * proj).reshape(ML_DEV, KNB, channels), axis=1) * (1.0 / KNB)
    update = jnp.dot(message.astype(jnp.bfloat16), mix[0], preferred_element_type=jnp.float32)
    feat1 = feat[EDGES : EDGES + ML_DEV] + update * lax.logistic(update)
    feat_out[:, :channels] = feat1
    feat_out[:, channels:] = jnp.broadcast_to(pot_of[EDGES : EDGES + ML_DEV], (ML_DEV, LANES))
    proj_out[...] = jnp.dot(feat1.astype(jnp.bfloat16), msg[1], preferred_element_type=jnp.float32).astype(jnp.bfloat16)


def first_layer(*args):
    channels = args[7].shape[1]
    smem = pl.BlockSpec(memory_space=pltpu.SMEM)
    vmem = pl.BlockSpec(memory_space=pltpu.VMEM)
    return pl.pallas_call(
        first_layer_kernel,
        out_shape=(
            jax.ShapeDtypeStruct((ML_DEV, channels + LANES), jnp.float32),
            jax.ShapeDtypeStruct((ML_DEV, channels), jnp.bfloat16),
        ),
        in_specs=[smem] + [vmem] * 9,
        out_specs=(vmem,) * 2,
        compiler_params=vmem_mib(20),
        name="first_layer",
    )(*args)


def fetch(sources, places, sems):
    copies = [pltpu.make_async_copy(src, dst, sems.at[i]) for i, (src, dst) in enumerate(zip(sources, places))]
    for copy in copies:
        copy.start()
    return copies


def second_layer_kernel(
    me, ids_in, basis_in, feat1, radial_in, mix_in, charge_w, energy_w, p0, p1, p2, p3, p4, p5, p6, p7,
    charge_out, energy_out, proj, ids, basis, feat_v, radial_w, mix, charge_v, energy_v, sems,
):
    parts = (p0, p1, p2, p3, p4, p5, p6, p7)
    size = p0.shape[0]
    copies = fetch(
        (ids_in, basis_in, feat1, radial_in, mix_in, charge_w, energy_w) + parts,
        [ids, basis, feat_v, radial_w, mix, charge_v, energy_v]
        + [proj.at[pl.ds(i * size, size)] for i in range(8)],
        sems,
    )
    copies[0].wait()
    part = 256
    mine = me[0]
    messages = []
    for m in range(EDGES // part):
        here = slice(m * part, (m + 1) * part)
        atom = ids[here, :]
        dev = (atom * 52429) >> 21
        t = atom - dev * ML_DEV
        far_c = (mine ^ dev) & 1
        far_z = ((mine >> 2) - (dev >> 2)) & 3
        far_x = ((mine >> 5) - (dev >> 5)) & 3
        row_of = lambda v: 2 * ((v >> 4) & 1) + ((v >> 1) & 1)
        far_y = (row_of(mine) - row_of(dev)) & 3
        place = ((far_c * 4 + far_y) * 16 + far_x * 4 + far_z) * ML_DEV + t
        pick = (lane_iota((part, 8 * size)) == place).astype(jnp.float32).astype(jnp.bfloat16)
        if m == 0:
            for copy in copies[1:]:
                copy.wait()
        rows = jnp.dot(pick, proj[...], preferred_element_type=jnp.float32)
        radial = radial_of(basis[here, :], radial_w[1])
        messages.append(jnp.sum((radial * rows).reshape(part // KNB, KNB, rows.shape[1]), axis=1) * (1.0 / KNB))
    message = jnp.concatenate(messages, axis=0).astype(jnp.bfloat16)
    update = jnp.dot(message, mix[1], preferred_element_type=jnp.float32)
    channels = update.shape[1]
    feat = feat_v[:, :channels] + update * lax.logistic(update)
    charge = jnp.tanh(jnp.sum(feat * charge_v[...], axis=1, keepdims=True))
    energy = jnp.sum(feat * energy_v[...], axis=1, keepdims=True) + charge * feat_v[:, channels : channels + 1]

    def as_row(column):
        square = jnp.broadcast_to(column, (ML_DEV, LANES))
        return jnp.concatenate([square, jnp.zeros((LANES - ML_DEV, LANES), jnp.float32)], axis=0).T

    charge_out[...] = as_row(charge)
    energy_out[...] = as_row(energy)[:1]


def second_layer(*args):
    smem = pl.BlockSpec(memory_space=pltpu.SMEM)
    vmem = pl.BlockSpec(memory_space=pltpu.VMEM)
    like = lambda a: pltpu.VMEM(a.shape, a.dtype)
    parts = args[8:]
    rows, channels = parts[0].shape
    return pl.pallas_call(
        second_layer_kernel,
        out_shape=(
            jax.ShapeDtypeStruct((NDEV, LANES), jnp.float32),
            pltpu.HBM((1, LANES), jnp.float32),
        ),
        in_specs=[smem] + [pl.BlockSpec(memory_space=pltpu.HBM)] * 15,
        out_specs=(vmem,) * 2,
        scratch_shapes=[pltpu.VMEM((8 * rows, channels), jnp.bfloat16)]
        + [like(a) for a in args[1:8]]
        + [pltpu.SemaphoreType.DMA((15,))],
        compiler_params=vmem_mib(24),
        name="second_layer",
    )(*args)


def embed_kernel(scale, mm, tab, charges, blocks_in, count_in, atoms_in, slots_in, *rest):
    pieces, (out, c8, left, total, blocks, count, atoms, slots, sems) = rest[:-9], rest[-9:]
    begins = [sum(piece.shape[1] for piece in pieces[:i]) for i in range(len(pieces))]
    copies = fetch(
        (atoms_in, slots_in, blocks_in, count_in) + pieces,
        [atoms, slots, blocks, count]
        + [out.at[:, pl.ds(begin, piece.shape[1])] for begin, piece in zip(begins, pieces)],
        sems,
    )
    turned = tab[:, :LANES].T
    charge = charges[...].T[:ML_DEV]
    c8[...] = jnp.zeros_like(c8)
    c8[pl.ds(0, ML_DEV, stride=8), :] = charge
    for c in range(3):
        c8[pl.ds(c + 1, ML_DEV, stride=8), :] = charge * turned[ML_DEV * c : ML_DEV * (c + 1)]

    def charge_tile(t, carry):
        one, two, _ = three_parts(c8[pl.ds(pl.multiple_of(t * 8, 8), 8), :])
        left[:, pl.ds(pl.multiple_of(t * LANES, LANES), LANES)] = jnp.concatenate([one, two], axis=0).astype(
            jnp.bfloat16
        )
        return carry

    lax.fori_loop(0, ML_DEV, charge_tile, 0)
    nslots = blocks.shape[1]
    total[...] = jnp.zeros_like(total)
    copies[0].wait()
    copies[1].wait()

    def tile(i, carry):
        cols = pl.ds(pl.multiple_of(i * 256, 256), 256)
        some = atoms[:, cols]
        lhs = left[:, cols]
        for s in range(nslots // 2):
            inv = lax.rsqrt(rows0(some, slots[:, s * 256 : (s + 1) * 256]))
            cube = inv * inv * inv
            high = cube.astype(jnp.bfloat16)
            low = (cube - high.astype(jnp.float32)).astype(jnp.bfloat16)
            total[:, s * 256 : (s + 1) * 256] += jnp.dot(lhs, high, preferred_element_type=jnp.float32) + jnp.dot(
                lhs, low, preferred_element_type=jnp.float32
            )
        return carry

    lax.fori_loop(0, ML_DEV // 2, tile, 0, unroll=10)
    for copy in copies[2:]:
        copy.wait()
    for s in range(nslots):
        here = pl.ds(pl.multiple_of(blocks[0, s] * LANES, LANES), LANES)
        rows = mm[:, here]
        q = rows[3:4] * (scale * jnp.where(s < count[0], 1.0, 0.0))
        sums = total[:, s * LANES : (s + 1) * LANES]
        sums = sums[:8] + sums[8:]
        out[:, here] += q * (rows[:3] * sums[0:1] - sums[1:4])


def embed(blocks, count, mm, tab, charges, atoms, slots, pieces, scale):
    vmem = pl.BlockSpec(memory_space=pltpu.VMEM)
    return pl.pallas_call(
        functools.partial(embed_kernel, scale),
        out_shape=jax.ShapeDtypeStruct((3, mm.shape[1]), jnp.float32),
        in_specs=[vmem] * 3 + [pl.BlockSpec(memory_space=pltpu.HBM)] * (4 + len(pieces)),
        out_specs=vmem,
        scratch_shapes=[
            pltpu.VMEM((8 * ML_DEV, LANES), jnp.float32),
            pltpu.VMEM((16, ML_DEV * LANES), jnp.bfloat16),
            pltpu.VMEM((16, slots.shape[1]), jnp.float32),
            pltpu.SMEM(blocks.shape, blocks.dtype),
            pltpu.SMEM(count.shape, count.dtype),
            pltpu.VMEM(atoms.shape, atoms.dtype),
            pltpu.VMEM(slots.shape, slots.dtype),
            pltpu.SemaphoreType.DMA((4 + len(pieces),)),
        ],
        compiler_params=vmem_mib(12),
        name="embed_forces",
    )(mm, tab, charges, blocks, count, atoms, slots, *pieces)


def ring_parts(value, axis):
    n = lax.axis_size(axis)
    return [value] + [lax.ppermute(value, axis, [(i, (i + k) % n) for i in range(n)]) for k in range(1, n)]


def stand(value, zero):
    return value + zero[:, : value.shape[1]].astype(value.dtype)


def body(
    mm_atoms,
    neighbours,
    embed_blocks,
    embed_count,
    ml_coords,
    ml_species,
    ml_edges,
    species_table,
    field_weight,
    msg_weight,
    radial_weight,
    mix_weight,
    charge_weight,
    energy_weight,
):
    own_rows = mm_atoms.shape[1]
    kappa = 4.0 / math.sqrt(NDEV * ML_DEV)
    kappa_field = 3.0 / math.sqrt(NDEV * embed_blocks.shape[1] * LANES)
    me = lax.axis_index(ALL)[None]
    tab = lax.all_to_all(spread(ml_coords, ml_species[None]), ALL, 0, 0, tiled=True)
    tab = tab.reshape(NDEV, 2 * LANES)
    ids = ml_edges.reshape(-1, 1)
    blocks = own_rows // LANES
    cuts = (0, 12, 48, 56, 64, 72, 88, blocks - 12, blocks)
    far = ml_coords

    def pairs(i, after, before=far, behind=far):
        return pair_forces(cuts[i], cuts[i + 1] - cuts[i], before, mm_atoms, behind, neighbours, after)

    pieces = [None] * (len(cuts) - 1)
    pieces[1], zero = pairs(1, far)
    pot, atoms, slots = field(embed_blocks, embed_count, mm_atoms, tab, pieces[1], kappa_field)
    basis, kinds, zero = geometry(me, ids, tab, pot)
    pot = stand(functools.reduce(jnp.add, ring_parts(pot, "z")), zero)
    for i, axis in ((2, Y), (3, "x")):
        pieces[i], zero = pairs(i, pot)
        pot = stand(functools.reduce(jnp.add, ring_parts(pot, axis)), zero)
    pot = functools.reduce(jnp.add, ring_parts(pot, "c"))
    feat1, proj = first_layer(
        me, ids, pot, basis, kinds, species_table, field_weight[None], msg_weight, radial_weight, mix_weight
    )
    for i, axis in ((4, "z"), (5, "x")):
        pieces[i], zero = pairs(i, proj)
        proj = stand(jnp.concatenate(ring_parts(proj, axis), axis=0), zero)
    halo = HALO_BLOCKS * LANES
    up = [(i, (i + 1) % NDEV) for i in range(NDEV)]
    down = [(j, i) for i, j in up]
    before = lax.ppermute(stand(mm_atoms[:, own_rows - halo :], zero), ALL, up)
    behind = lax.ppermute(stand(mm_atoms[:, :halo], zero), ALL, down)
    pieces[6], zero = pairs(6, proj)
    parts = ring_parts(proj, Y)
    parts[1:] = [stand(part, zero) for part in parts[1:]]
    parts = parts + [ring_parts(part, "c")[1] for part in parts]
    charges, energy = second_layer(
        me,
        ids,
        basis,
        feat1,
        radial_weight,
        mix_weight,
        charge_weight[None],
        energy_weight[None],
        *parts,
    )
    for i in (0, 7):
        pieces[i], _ = pairs(i, charges, before, behind)
    charges = lax.all_to_all(charges, ALL, 0, 0, tiled=True)
    mm_force = embed(embed_blocks, embed_count, mm_atoms, tab, charges, atoms, slots, pieces, kappa)
    return (energy[0, :ML_DEV], mm_force)


def solution(mesh):
    fine = Mesh(mesh.devices.reshape(4, 2, 4, 2, 2), ALL)
    in_specs = (
        P(None, ALL),
        P(None, ALL),
        P(ALL, None),
        P(ALL),
        P(None, ALL),
        P(ALL),
        P(ALL, None),
        P(),
        P(),
        P(),
        P(),
        P(),
        P(),
        P(),
    )
    out_specs = (P(ALL), P(None, ALL))
    return jax.shard_map(body, mesh=fine, in_specs=in_specs, out_specs=out_specs, check_vma=False)
```

```python
import functools
import math

import jax
import jax.numpy as jnp
from jax import lax
from jax.experimental import pallas as pl
from jax.experimental.pallas import tpu as pltpu
from jax.sharding import Mesh
from jax.sharding import PartitionSpec as P

ALL = ("x", "yh", "z", "yl", "c")
STAGES = ((2, 0, 1), (0, 1, 2))
vmem_mib = lambda size: pltpu.CompilerParams(vmem_limit_bytes=size * 1024 * 1024)
LANES = 128
NDEV = 128
ML_DEV = 40
KNB = 32
EDGES = ML_DEV * KNB
ROWS = 1344
HALO_BLOCKS = 8
PAIR_STEP = 4


def rows0(left, right):
    return lax.dot_general(
        left, right, (((0,), (0,)), ((), ())), preferred_element_type=jnp.float32
    )


def pair_kernel(first, count, left, own, right, nb, *rest):
    out, zero, ext = rest[-3:]
    own_blocks = own.shape[1] // LANES
    step = pl.program_id(0)

    @pl.when(step == 0)
    def _():
        zero[...] = jnp.zeros_like(zero)
        low, high = first - HALO_BLOCKS, first + count + HALO_BLOCKS
        for src, begin, size in ((left, -HALO_BLOCKS, HALO_BLOCKS), (own, 0, own_blocks), (right, own_blocks, HALO_BLOCKS)):
            start, stop = max(low, begin), min(high, begin + size)
            if start >= stop:
                continue

            def fill(r, carry, src=src, begin=begin):
                rows = src[:, pl.ds(pl.multiple_of((r - begin) * LANES, LANES), LANES)]
                for c in range(4):
                    ext[c, r - low] = jnp.broadcast_to(rows[c : c + 1], (8, LANES))
                return carry

            lax.fori_loop(start, stop, fill, 0)

    blocks = nb.shape[1] // LANES

    def block(j, carry):
        b = step * blocks + j
        lanes = pl.ds(pl.multiple_of(j * LANES, LANES), LANES)
        rel = nb[:, lanes] - (b + first) * LANES
        row = rel >> 7
        lane = rel & 127
        centre = [ext[c, b + HALO_BLOCKS] for c in range(4)]
        total = [jnp.zeros((8, LANES), jnp.float32) for _ in range(3)]
        for h in range(nb.shape[0] // 8):
            near = row[8 * h : 8 * h + 8]
            pick = lane[8 * h : 8 * h + 8]
            got = [jnp.zeros((8, LANES), jnp.float32) for _ in range(4)]
            for k in range(2 * HALO_BLOCKS + 1):
                here = near == k
                for c in range(4):
                    value = jnp.take_along_axis(ext[c, b + k], pick, axis=1, mode="promise_in_bounds")
                    got[c] = jnp.where(here, value, got[c])
            off = [centre[c] - got[c] for c in range(3)]
            inv = lax.rsqrt(off[0] * off[0] + off[1] * off[1] + off[2] * off[2] + 1.0)
            strength = centre[3] * got[3] * (inv * inv * inv)
            for c in range(3):
                total[c] = total[c] + strength * off[c]
        for c in range(3):
            out[c : c + 1, lanes] = jnp.sum(total[c], axis=0, keepdims=True)
        return carry

    lax.fori_loop(0, blocks, block, 0, unroll=PAIR_STEP)


def pair_forces(first, count, left, own, right, neighbours, after):
    wide = PAIR_STEP * LANES
    whole = lambda a: pl.BlockSpec(a.shape, lambda i: (0, 0))
    slots = neighbours.shape[0]
    return pl.pallas_call(
        functools.partial(pair_kernel, first, count),
        grid=(count // PAIR_STEP,),
        out_shape=(
            jax.ShapeDtypeStruct((3, count * LANES), jnp.float32),
            jax.ShapeDtypeStruct((1, HALO_BLOCKS * LANES), jnp.float32),
        ),
        in_specs=[
            whole(left),
            whole(own),
            whole(right),
            pl.BlockSpec((slots, wide), lambda i: (0, i + first // PAIR_STEP)),
            *[pl.BlockSpec(memory_space=pl.ANY)] * len(after),
        ],
        out_specs=(
            pl.BlockSpec((3, wide), lambda i: (0, i)),
            pl.BlockSpec((1, HALO_BLOCKS * LANES), lambda i: (0, 0)),
        ),
        scratch_shapes=[pltpu.VMEM((4, count + 2 * HALO_BLOCKS, 8, LANES), jnp.float32)],
        compiler_params=vmem_mib(6),
        cost_estimate=pl.CostEstimate(
            flops=count * 10**7, bytes_accessed=count * 16384, transcendentals=count * slots * LANES
        ),
        name="pair_forces",
    )(left, own, right, neighbours, *after)


def spread_kernel(coords, species, out):
    rows = [coords[c : c + 1, :] for c in range(3)] + [species[...].astype(jnp.float32)]
    rows = rows[:3] + [jnp.zeros((1, 8), jnp.float32)] + rows[3:] + [jnp.zeros((1, LANES - ML_DEV), jnp.float32)]
    out[:, 0, :] = jnp.broadcast_to(jnp.concatenate(rows, axis=1), (NDEV, 2 * LANES))


def spread(coords, species):
    vmem = pl.BlockSpec(memory_space=pltpu.VMEM)
    return pl.pallas_call(
        spread_kernel,
        out_shape=jax.ShapeDtypeStruct((NDEV, 1, 2 * LANES), jnp.float32),
        in_specs=[vmem, vmem],
        out_specs=vmem,
        name="spread",
    )(coords, species)


def three_parts(value):
    one = value.astype(jnp.bfloat16).astype(jnp.float32)
    rest = value - one
    two = rest.astype(jnp.bfloat16).astype(jnp.float32)
    three = (rest - two).astype(jnp.bfloat16).astype(jnp.float32)
    return one, two, three


def field_kernel(scale, blocks_in, count_in, mm, tab, after, pot, atoms, slots, p8, qb, blocks, count, sems):
    copies = fetch((blocks_in, count_in), (blocks, count), sems)
    turned = tab[:, :LANES].T
    x, y, z = (turned[ML_DEV * c : ML_DEV * (c + 1)] for c in range(3))
    p8[...] = jnp.zeros_like(p8)
    for c, value in enumerate((x, y, z, x * x + y * y + z * z, jnp.ones_like(x))):
        p8[pl.ds(c, ML_DEV, stride=8), :] = value

    def atom_tile(t, carry):
        one, two, three = three_parts(p8[pl.ds(pl.multiple_of(t * 8, 8), 8), :])
        atoms[:, pl.ds(pl.multiple_of(t * LANES, LANES), LANES)] = jnp.concatenate(
            [one, one, two, two, one, three], axis=0
        ).astype(jnp.bfloat16)
        return carry

    lax.fori_loop(0, ML_DEV, atom_tile, 0)
    for copy in copies:
        copy.wait()
    nslots = blocks.shape[1]
    for s in range(nslots):
        rows = mm[:, pl.ds(pl.multiple_of(blocks[0, s] * LANES, LANES), LANES)]
        q = rows[3:4] * jnp.where(s < count[0], 1.0, 0.0)
        pos = rows[:3]
        norm = jnp.sum(pos * pos, axis=0, keepdims=True) + 1.0
        eight = jnp.concatenate(
            [-2.0 * pos, jnp.ones_like(q), norm, jnp.zeros((3, LANES), jnp.float32)], axis=0
        )
        one, two, three = three_parts(eight)
        slots[:, s * LANES : (s + 1) * LANES] = jnp.concatenate(
            [one, two, one, two, three, one], axis=0
        ).astype(jnp.bfloat16)
        qb[s * LANES : (s + 1) * LANES, :] = jnp.broadcast_to(q, (LANES, LANES)).T

    def tile(i, carry):
        right = atoms[:, pl.ds(pl.multiple_of(i * 256, 256), 256)]
        total = jnp.zeros((8, 256), jnp.float32)
        for s in range(nslots // 2):
            inv = lax.rsqrt(rows0(slots[:, s * 256 : (s + 1) * 256], right))
            q = qb[s * 256 : (s + 1) * 256, :]
            term = inv * jnp.concatenate([q, q], axis=1)
            total = total + jnp.sum(term.reshape(32, 8, 256), axis=0)
        total = scale * jnp.sum(total, axis=0, keepdims=True)
        pot[pl.ds(2 * i, 1), :] = total[:, :LANES]
        pot[pl.ds(2 * i + 1, 1), :] = total[:, LANES:]
        return carry

    lax.fori_loop(0, ML_DEV // 2, tile, 0, unroll=5)


def field(blocks, count, mm, tab, after, scale):
    nslots = blocks.shape[1]
    hbm = pl.BlockSpec(memory_space=pltpu.HBM)
    vmem = pl.BlockSpec(memory_space=pltpu.VMEM)
    return pl.pallas_call(
        functools.partial(field_kernel, scale),
        out_shape=(
            jax.ShapeDtypeStruct((ML_DEV, LANES), jnp.float32),
            pltpu.HBM((48, ML_DEV * LANES), jnp.bfloat16),
            pltpu.HBM((48, nslots * LANES), jnp.bfloat16),
        ),
        in_specs=[hbm, hbm, vmem, vmem, pl.BlockSpec(memory_space=pl.ANY)],
        out_specs=(vmem,) * 3,
        scratch_shapes=[
            pltpu.VMEM((8 * ML_DEV, LANES), jnp.float32),
            pltpu.VMEM((nslots * LANES, LANES), jnp.float32),
            pltpu.SMEM(blocks.shape, blocks.dtype),
            pltpu.SMEM(count.shape, count.dtype),
            pltpu.SemaphoreType.DMA((2,)),
        ],
        compiler_params=vmem_mib(10),
        name="field",
    )(blocks, count, mm, tab, after)


def lane_iota(shape):
    return lax.broadcasted_iota(jnp.int32, shape, 1)


def exact_pick(left, right):
    left = left.astype(jnp.bfloat16)
    parts = [jnp.dot(left, part.astype(jnp.bfloat16), preferred_element_type=jnp.float32) for part in three_parts(right)]
    return (parts[2] + parts[1]) + parts[0]


def exact_sum(left, right):
    right = right.astype(jnp.bfloat16)
    parts = [jnp.dot(part.astype(jnp.bfloat16), right, preferred_element_type=jnp.float32) for part in three_parts(left)]
    return (parts[2] + parts[1]) + parts[0]


def where_is(me, ids):
    own_ids = me * ML_DEV + jnp.minimum(lax.broadcasted_iota(jnp.int32, (ROWS - EDGES, 1), 0), ML_DEV - 1)
    atom = jnp.concatenate([ids, own_ids], axis=0)
    dev = (atom * 52429) >> 21
    return dev, atom - dev * ML_DEV


def geometry_kernel(me, ids, tab, field_w, charge_w, energy_w, after, basis_out, kinds_out, rows_out, zero):
    zero[...] = jnp.zeros_like(zero)
    rows_out[...] = jnp.concatenate([field_w[...], charge_w[...], energy_w[...], field_w[...]], axis=0)
    dev, t = where_is(me[0], ids[...])
    at_dev = lane_iota((ROWS, LANES)) == dev
    rows = exact_pick(jnp.where(at_dev, 1.0, 0.0), tab[...])
    lane = lane_iota((1, 2 * LANES))
    place = jnp.where(lane < ML_DEV, lane, jnp.where(lane < 2 * ML_DEV, lane - ML_DEV, lane - 2 * ML_DEV))
    place = jnp.where(lane < LANES, place, lane - LANES)
    place = jnp.where(place < ML_DEV, place, -1)
    rows = jnp.where(place == t, rows, 0.0)
    src = lax.broadcasted_iota(jnp.int32, (2 * LANES, LANES), 0)
    dst = lane_iota((2 * LANES, LANES))
    group = jnp.where(src < ML_DEV, 0, jnp.where(src < 2 * ML_DEV, 1, jnp.where(src < LANES, 2, 3)))
    picked = exact_sum(rows, jnp.where(group == dst, 1.0, 0.0))
    own = picked[EDGES : EDGES + ML_DEV]
    centre = jnp.broadcast_to(own[:, None, :], (ML_DEV, KNB, LANES)).reshape(EDGES, LANES)
    gap = picked[:EDGES] - centre
    lanes = lane_iota((EDGES, LANES))
    dist = jnp.sqrt(exact_sum(jnp.where(lanes < 3, gap * gap, 0.0), jnp.ones((LANES, LANES), jnp.float32)))
    shift = dist - 0.5 * (lanes & 7).astype(jnp.float32)
    one, two, three = three_parts(jnp.exp(-2.0 * (shift * shift)))
    part = lanes >> 3
    value = jnp.where((part < 2) | (part == 4), one, jnp.where(part < 4, two, three))
    basis_out[...] = jnp.where(part < 6, value, 0.0).astype(jnp.bfloat16)
    kind = jnp.broadcast_to(picked[:, 3:4], (ROWS, LANES)).astype(jnp.int32)
    lanes = lane_iota((ROWS, LANES))
    kinds_out[...] = jnp.where((kind == (lanes & 15)) & (lanes < 48), 1.0, 0.0).astype(jnp.bfloat16)


def geometry(me, ids, tab, field_w, charge_w, energy_w, after):
    smem = pl.BlockSpec(memory_space=pltpu.SMEM)
    vmem = pl.BlockSpec(memory_space=pltpu.VMEM)
    return pl.pallas_call(
        geometry_kernel,
        out_shape=(
            jax.ShapeDtypeStruct((EDGES, LANES), jnp.bfloat16),
            jax.ShapeDtypeStruct((ROWS, LANES), jnp.bfloat16),
            jax.ShapeDtypeStruct((4, field_w.shape[1]), jnp.float32),
            jax.ShapeDtypeStruct((1, LANES), jnp.float32),
        ),
        in_specs=[smem] + [vmem] * 5 + [pl.BlockSpec(memory_space=pl.ANY)],
        out_specs=(vmem,) * 4,
        compiler_params=vmem_mib(20),
        name="geometry",
    )(me, ids, tab, field_w, charge_w, energy_w, after)


def radial_of(basis, weights):
    one, two, three = three_parts(weights)
    rest = jnp.zeros((LANES - 48, weights.shape[1]), jnp.float32)
    stacked = jnp.concatenate([one, two, one, two, three, one, rest], axis=0).astype(jnp.bfloat16)
    return jnp.dot(basis, stacked, preferred_element_type=jnp.float32)


def first_layer_kernel(
    me, ids, pot, basis, kinds, table, field_w, msg, radial_w, mix, feat_out, proj_out
):
    pot_rows = jnp.concatenate([pot[...], jnp.zeros((LANES - ML_DEV, LANES), jnp.float32)], axis=0).T
    dev, t = where_is(me[0], ids[...])
    lanes = lane_iota((ROWS, LANES))
    rows = exact_pick(jnp.where(lanes == dev, 1.0, 0.0), pot_rows)
    pot_of = jnp.sum(jnp.where(lanes == t, rows, 0.0), axis=1, keepdims=True)
    channels = msg.shape[1]
    lines = jnp.concatenate([table[...], jnp.zeros((16 - table.shape[0], channels), jnp.float32)], axis=0)
    lines = jnp.concatenate(three_parts(lines) + (jnp.zeros((LANES - 48, channels), jnp.float32),), axis=0)
    feat = jnp.dot(kinds[...], lines.astype(jnp.bfloat16), preferred_element_type=jnp.float32)
    feat = feat + pot_of * field_w[:1]
    proj = jnp.dot(feat[:EDGES].astype(jnp.bfloat16), msg[0], preferred_element_type=jnp.float32)
    proj = proj.astype(jnp.bfloat16).astype(jnp.float32)
    radial = radial_of(basis[...], radial_w[0])
    message = jnp.sum((radial * proj).reshape(ML_DEV, KNB, channels), axis=1) * (1.0 / KNB)
    update = jnp.dot(message.astype(jnp.bfloat16), mix[0], preferred_element_type=jnp.float32)
    feat1 = feat[EDGES : EDGES + ML_DEV] + update * lax.logistic(update)
    feat_out[:, :channels] = feat1
    feat_out[:, channels:] = jnp.broadcast_to(pot_of[EDGES : EDGES + ML_DEV], (ML_DEV, LANES))
    proj_out[...] = jnp.dot(feat1.astype(jnp.bfloat16), msg[1], preferred_element_type=jnp.float32).astype(jnp.bfloat16)


def first_layer(*args):
    channels = args[7].shape[1]
    smem = pl.BlockSpec(memory_space=pltpu.SMEM)
    vmem = pl.BlockSpec(memory_space=pltpu.VMEM)
    return pl.pallas_call(
        first_layer_kernel,
        out_shape=(
            jax.ShapeDtypeStruct((ML_DEV, channels + LANES), jnp.float32),
            jax.ShapeDtypeStruct((ML_DEV, channels), jnp.bfloat16),
        ),
        in_specs=[smem] + [vmem] * 9,
        out_specs=(vmem,) * 2,
        compiler_params=vmem_mib(20),
        name="first_layer",
    )(*args)


def fetch(sources, places, sems):
    copies = [pltpu.make_async_copy(src, dst, sems.at[i]) for i, (src, dst) in enumerate(zip(sources, places))]
    for copy in copies:
        copy.start()
    return copies


def second_layer_kernel(
    me, ids_in, basis_in, feat1, radial_in, mix_in, rows_in, p0, p1, p2, p3, p4, p5, p6, p7,
    charge_out, energy_out, proj, ids, basis, feat_v, radial_w, mix, lines, sems,
):
    parts = (p0, p1, p2, p3, p4, p5, p6, p7)
    size = p0.shape[0]
    copies = fetch(
        (ids_in, basis_in, feat1, radial_in, mix_in, rows_in) + parts,
        [ids, basis, feat_v, radial_w, mix, lines]
        + [proj.at[pl.ds(i * size, size)] for i in range(8)],
        sems,
    )
    copies[0].wait()
    part = 256
    mine = me[0]
    messages = []
    for m in range(EDGES // part):
        here = slice(m * part, (m + 1) * part)
        atom = ids[here, :]
        dev = (atom * 52429) >> 21
        t = atom - dev * ML_DEV
        far_c = (mine ^ dev) & 1
        far_z = ((mine >> 2) - (dev >> 2)) & 3
        far_x = ((mine >> 5) - (dev >> 5)) & 3
        row_of = lambda v: 2 * ((v >> 4) & 1) + ((v >> 1) & 1)
        far_y = (row_of(mine) - row_of(dev)) & 3
        odd = (dev & 1) == 1
        far = (far_x, far_y, far_z)
        k1, k2, k3 = (jnp.where(odd, far[STAGES[1][i]], far[STAGES[0][i]]) for i in range(3))
        place = ((far_c * 4 + k3) * 16 + k2 * 4 + k1) * ML_DEV + t
        same = lane_iota((part, 8 * size)).astype(jnp.int16) == place.astype(jnp.int16)
        pick = jnp.where(same, jnp.bfloat16(1), jnp.bfloat16(0))
        if m == 0:
            for copy in copies[1:]:
                copy.wait()
        rows = jnp.dot(pick, proj[...], preferred_element_type=jnp.float32)
        radial = radial_of(basis[here, :], radial_w[1])
        messages.append(jnp.sum((radial * rows).reshape(part // KNB, KNB, rows.shape[1]), axis=1) * (1.0 / KNB))
    message = jnp.concatenate(messages, axis=0).astype(jnp.bfloat16)
    update = jnp.dot(message, mix[1], preferred_element_type=jnp.float32)
    channels = update.shape[1]
    feat = feat_v[:, :channels] + update * lax.logistic(update)
    charge = jnp.tanh(jnp.sum(feat * lines[1:2], axis=1, keepdims=True))
    energy = jnp.sum(feat * lines[2:3], axis=1, keepdims=True) + charge * feat_v[:, channels : channels + 1]

    def as_row(column):
        square = jnp.broadcast_to(column, (ML_DEV, LANES))
        return jnp.concatenate([square, jnp.zeros((LANES - ML_DEV, LANES), jnp.float32)], axis=0).T

    charge_out[...] = as_row(charge)
    energy_out[...] = as_row(energy)[:1]


def second_layer(*args):
    smem = pl.BlockSpec(memory_space=pltpu.SMEM)
    vmem = pl.BlockSpec(memory_space=pltpu.VMEM)
    like = lambda a: pltpu.VMEM(a.shape, a.dtype)
    parts = args[7:]
    rows, channels = parts[0].shape
    return pl.pallas_call(
        second_layer_kernel,
        out_shape=(
            jax.ShapeDtypeStruct((NDEV, LANES), jnp.float32),
            pltpu.HBM((1, LANES), jnp.float32),
        ),
        in_specs=[smem] + [pl.BlockSpec(memory_space=pltpu.HBM)] * 14,
        out_specs=(vmem,) * 2,
        scratch_shapes=[pltpu.VMEM((8 * rows, channels), jnp.bfloat16)]
        + [like(a) for a in args[1:7]]
        + [pltpu.SemaphoreType.DMA((14,))],
        compiler_params=vmem_mib(24),
        name="second_layer",
    )(*args)


def embed_kernel(scale, mm, tab, charges, blocks_in, count_in, atoms_in, slots_in, *rest):
    pieces, (out, c8, left, total, blocks, count, atoms, slots, sems) = rest[:-9], rest[-9:]
    begins = [sum(piece.shape[1] for piece in pieces[:i]) for i in range(len(pieces))]
    copies = fetch(
        (atoms_in, slots_in, blocks_in, count_in) + pieces,
        [atoms, slots, blocks, count]
        + [out.at[:, pl.ds(begin, piece.shape[1])] for begin, piece in zip(begins, pieces)],
        sems,
    )
    turned = tab[:, :LANES].T
    charge = charges[...].T[:ML_DEV]
    c8[...] = jnp.zeros_like(c8)
    c8[pl.ds(0, ML_DEV, stride=8), :] = charge
    for c in range(3):
        c8[pl.ds(c + 1, ML_DEV, stride=8), :] = charge * turned[ML_DEV * c : ML_DEV * (c + 1)]

    def charge_tile(t, carry):
        one, two, _ = three_parts(c8[pl.ds(pl.multiple_of(t * 8, 8), 8), :])
        left[:, pl.ds(pl.multiple_of(t * LANES, LANES), LANES)] = jnp.concatenate([one, two], axis=0).astype(
            jnp.bfloat16
        )
        return carry

    lax.fori_loop(0, ML_DEV, charge_tile, 0)
    nslots = blocks.shape[1]
    total[...] = jnp.zeros_like(total)
    copies[0].wait()
    copies[1].wait()

    def tile(i, carry):
        cols = pl.ds(pl.multiple_of(i * 256, 256), 256)
        some = atoms[:, cols]
        lhs = left[:, cols]
        for s in range(nslots // 2):
            inv = lax.rsqrt(rows0(some, slots[:, s * 256 : (s + 1) * 256]))
            cube = inv * inv * inv
            high = cube.astype(jnp.bfloat16)
            low = (cube - high.astype(jnp.float32)).astype(jnp.bfloat16)
            total[:, s * 256 : (s + 1) * 256] += jnp.dot(lhs, high, preferred_element_type=jnp.float32) + jnp.dot(
                lhs, low, preferred_element_type=jnp.float32
            )
        return carry

    lax.fori_loop(0, ML_DEV // 2, tile, 0, unroll=10)
    for copy in copies[2:]:
        copy.wait()
    for s in range(nslots):
        here = pl.ds(pl.multiple_of(blocks[0, s] * LANES, LANES), LANES)
        rows = mm[:, here]
        q = rows[3:4] * (scale * jnp.where(s < count[0], 1.0, 0.0))
        sums = total[:, s * LANES : (s + 1) * LANES]
        sums = sums[:8] + sums[8:]
        out[:, here] += q * (rows[:3] * sums[0:1] - sums[1:4])


def embed(blocks, count, mm, tab, charges, atoms, slots, pieces, scale):
    vmem = pl.BlockSpec(memory_space=pltpu.VMEM)
    return pl.pallas_call(
        functools.partial(embed_kernel, scale),
        out_shape=jax.ShapeDtypeStruct((3, mm.shape[1]), jnp.float32),
        in_specs=[vmem] * 3 + [pl.BlockSpec(memory_space=pltpu.HBM)] * (4 + len(pieces)),
        out_specs=vmem,
        scratch_shapes=[
            pltpu.VMEM((8 * ML_DEV, LANES), jnp.float32),
            pltpu.VMEM((16, ML_DEV * LANES), jnp.bfloat16),
            pltpu.VMEM((16, slots.shape[1]), jnp.float32),
            pltpu.SMEM(blocks.shape, blocks.dtype),
            pltpu.SMEM(count.shape, count.dtype),
            pltpu.VMEM(atoms.shape, atoms.dtype),
            pltpu.VMEM(slots.shape, slots.dtype),
            pltpu.SemaphoreType.DMA((4 + len(pieces),)),
        ],
        compiler_params=vmem_mib(12),
        name="embed_forces",
    )(mm, tab, charges, blocks, count, atoms, slots, *pieces)


def stage_parts(value, stage):
    parts = [value]
    for k in range(1, 4):
        pairs = []
        for dev in range(NDEV):
            at = [dev >> 5, 2 * ((dev >> 4) & 1) + ((dev >> 1) & 1), (dev >> 2) & 3]
            axis = STAGES[dev & 1][stage]
            at[axis] = (at[axis] + k) % 4
            x, y, z = at
            pairs.append((dev, (x << 5) + ((y >> 1) << 4) + (z << 2) + ((y & 1) << 1) + (dev & 1)))
        parts.append(lax.ppermute(value, ALL, pairs))
    return parts


def ring_parts(value, axis):
    n = lax.axis_size(axis)
    return [value] + [lax.ppermute(value, axis, [(i, (i + k) % n) for i in range(n)]) for k in range(1, n)]


def stand(value, zero):
    return value + zero[:, : value.shape[1]].astype(value.dtype)


def body(
    mm_atoms,
    neighbours,
    embed_blocks,
    embed_count,
    ml_coords,
    ml_species,
    ml_edges,
    species_table,
    field_weight,
    msg_weight,
    radial_weight,
    mix_weight,
    charge_weight,
    energy_weight,
):
    own_rows = mm_atoms.shape[1]
    kappa = 4.0 / math.sqrt(NDEV * ML_DEV)
    kappa_field = 3.0 / math.sqrt(NDEV * embed_blocks.shape[1] * LANES)
    me = lax.axis_index(ALL)[None]
    tab = lax.all_to_all(spread(ml_coords, ml_species[None]), ALL, 0, 0, tiled=True)
    tab = tab.reshape(NDEV, 2 * LANES)
    ids = ml_edges.reshape(-1, 1)
    blocks = own_rows // LANES
    cuts = (0, 12, 48, 56, 64, 80, blocks - 12, blocks)
    far = ml_coords

    def pairs(i, *after, before=far, behind=far):
        return pair_forces(cuts[i], cuts[i + 1] - cuts[i], before, mm_atoms, behind, neighbours, after)

    pieces = [None] * (len(cuts) - 1)
    pieces[1], zero = pairs(1, far)
    pot, atoms, slots = field(embed_blocks, embed_count, mm_atoms, tab, pieces[1], kappa_field)
    basis, kinds, rows, zero = geometry(
        me, ids, tab, field_weight[None], charge_weight[None], energy_weight[None], pot
    )
    pot = stand(functools.reduce(jnp.add, stage_parts(pot, 0)), zero)
    pot = functools.reduce(jnp.add, stage_parts(pot, 1))
    pieces[2], zero = pairs(2, pot)
    pot = stand(functools.reduce(jnp.add, stage_parts(pot, 2)), zero)
    pot = functools.reduce(jnp.add, ring_parts(pot, "c"))
    feat1, proj = first_layer(
        me, ids, pot, basis, kinds, species_table, rows, msg_weight, radial_weight, mix_weight
    )
    for i, stage in ((3, 0), (4, 1)):
        pieces[i], zero = pairs(i, proj)
        proj = stand(jnp.concatenate(stage_parts(proj, stage), axis=0), zero)
    halo = HALO_BLOCKS * LANES
    up = [(i, (i + 1) % NDEV) for i in range(NDEV)]
    down = [(j, i) for i, j in up]
    before = lax.ppermute(stand(mm_atoms[:, own_rows - halo :], zero), ALL, up)
    behind = lax.ppermute(stand(mm_atoms[:, :halo], zero), ALL, down)
    pieces[5], zero = pairs(5, proj)
    parts = stage_parts(proj, 2)
    parts[1:] = [stand(part, zero) for part in parts[1:]]
    parts = parts + [ring_parts(part, "c")[1] for part in parts]
    charges, energy = second_layer(
        me,
        ids,
        basis,
        feat1,
        radial_weight,
        mix_weight,
        rows,
        *parts,
    )
    for i in (0, 6):
        pieces[i], _ = pairs(i, charges, before=before, behind=behind)
    charges = lax.all_to_all(charges, ALL, 0, 0, tiled=True)
    mm_force = embed(embed_blocks, embed_count, mm_atoms, tab, charges, atoms, slots, pieces, kappa)
    return (energy[0, :ML_DEV], mm_force)


def solution(mesh):
    fine = Mesh(mesh.devices.reshape(4, 2, 4, 2, 2), ALL)
    in_specs = (
        P(None, ALL),
        P(None, ALL),
        P(ALL, None),
        P(ALL),
        P(None, ALL),
        P(ALL),
        P(ALL, None),
        P(),
        P(),
        P(),
        P(),
        P(),
        P(),
        P(),
    )
    out_specs = (P(ALL), P(None, ALL))
    return jax.shard_map(body, mesh=fine, in_specs=in_specs, out_specs=out_specs, check_vma=False)
```

```python
import functools
import math

import jax
import jax.numpy as jnp
from jax import lax
from jax.experimental import pallas as pl
from jax.experimental.pallas import tpu as pltpu
from jax.sharding import Mesh
from jax.sharding import PartitionSpec as P

ALL = ("x", "yh", "z", "yl", "c")
STAGES = ((2, 0, 1), (0, 1, 2))
vmem_mib = lambda size: pltpu.CompilerParams(vmem_limit_bytes=size * 1024 * 1024)
LANES = 128
NDEV = 128
ML_DEV = 40
KNB = 32
EDGES = ML_DEV * KNB
ROWS = 1344
HALO_BLOCKS = 8
PAIR_STEP = 4


def rows0(left, right):
    return lax.dot_general(
        left, right, (((0,), (0,)), ((), ())), preferred_element_type=jnp.float32
    )


def pair_kernel(first, count, left, own, right, nb, *rest):
    out, zero, ext = rest[-3:]
    own_blocks = own.shape[1] // LANES
    step = pl.program_id(0)

    @pl.when(step == 0)
    def _():
        zero[...] = jnp.zeros_like(zero)
        low, high = first - HALO_BLOCKS, first + count + HALO_BLOCKS
        for src, begin, size in ((left, -HALO_BLOCKS, HALO_BLOCKS), (own, 0, own_blocks), (right, own_blocks, HALO_BLOCKS)):
            start, stop = max(low, begin), min(high, begin + size)
            if start >= stop:
                continue

            def fill(r, carry, src=src, begin=begin):
                rows = src[:, pl.ds(pl.multiple_of((r - begin) * LANES, LANES), LANES)]
                for c in range(4):
                    ext[c, r - low] = jnp.broadcast_to(rows[c : c + 1], (8, LANES))
                return carry

            lax.fori_loop(start, stop, fill, 0)

    blocks = nb.shape[1] // LANES

    def block(j, carry):
        b = step * blocks + j
        lanes = pl.ds(pl.multiple_of(j * LANES, LANES), LANES)
        rel = nb[:, lanes] - (b + first) * LANES
        row = rel >> 7
        lane = rel & 127
        centre = [ext[c, b + HALO_BLOCKS] for c in range(4)]
        total = [jnp.zeros((8, LANES), jnp.float32) for _ in range(3)]
        for h in range(nb.shape[0] // 8):
            near = row[8 * h : 8 * h + 8]
            pick = lane[8 * h : 8 * h + 8]
            got = [jnp.zeros((8, LANES), jnp.float32) for _ in range(4)]
            for k in range(2 * HALO_BLOCKS + 1):
                here = near == k
                for c in range(4):
                    value = jnp.take_along_axis(ext[c, b + k], pick, axis=1, mode="promise_in_bounds")
                    got[c] = jnp.where(here, value, got[c])
            off = [centre[c] - got[c] for c in range(3)]
            inv = lax.rsqrt(off[0] * off[0] + off[1] * off[1] + off[2] * off[2] + 1.0)
            strength = centre[3] * got[3] * (inv * inv * inv)
            for c in range(3):
                total[c] = total[c] + strength * off[c]
        for c in range(3):
            out[c : c + 1, lanes] = jnp.sum(total[c], axis=0, keepdims=True)
        return carry

    lax.fori_loop(0, blocks, block, 0, unroll=PAIR_STEP)


def pair_forces(first, count, left, own, right, neighbours, after):
    wide = PAIR_STEP * LANES
    whole = lambda a: pl.BlockSpec(a.shape, lambda i: (0, 0))
    slots = neighbours.shape[0]
    return pl.pallas_call(
        functools.partial(pair_kernel, first, count),
        grid=(count // PAIR_STEP,),
        out_shape=(
            jax.ShapeDtypeStruct((3, count * LANES), jnp.float32),
            jax.ShapeDtypeStruct((1, HALO_BLOCKS * LANES), jnp.float32),
        ),
        in_specs=[
            whole(left),
            whole(own),
            whole(right),
            pl.BlockSpec((slots, wide), lambda i: (0, i + first // PAIR_STEP)),
            *[pl.BlockSpec(memory_space=pl.ANY)] * len(after),
        ],
        out_specs=(
            pl.BlockSpec((3, wide), lambda i: (0, i)),
            pl.BlockSpec((1, HALO_BLOCKS * LANES), lambda i: (0, 0)),
        ),
        scratch_shapes=[pltpu.VMEM((4, count + 2 * HALO_BLOCKS, 8, LANES), jnp.float32)],
        compiler_params=vmem_mib(6),
        cost_estimate=pl.CostEstimate(
            flops=count * 10**7, bytes_accessed=count * 16384, transcendentals=count * slots * LANES
        ),
        name="pair_forces",
    )(left, own, right, neighbours, *after)


def spread_kernel(coords, species, out):
    rows = [coords[c : c + 1, :] for c in range(3)] + [species[...].astype(jnp.float32)]
    rows = rows[:3] + [jnp.zeros((1, 8), jnp.float32)] + rows[3:] + [jnp.zeros((1, LANES - ML_DEV), jnp.float32)]
    out[:, 0, :] = jnp.broadcast_to(jnp.concatenate(rows, axis=1), (NDEV, 2 * LANES))


def spread(coords, species):
    vmem = pl.BlockSpec(memory_space=pltpu.VMEM)
    return pl.pallas_call(
        spread_kernel,
        out_shape=jax.ShapeDtypeStruct((NDEV, 1, 2 * LANES), jnp.float32),
        in_specs=[vmem, vmem],
        out_specs=vmem,
        name="spread",
    )(coords, species)


def three_parts(value):
    one = value.astype(jnp.bfloat16).astype(jnp.float32)
    rest = value - one
    two = rest.astype(jnp.bfloat16).astype(jnp.float32)
    three = (rest - two).astype(jnp.bfloat16).astype(jnp.float32)
    return one, two, three


def field_kernel(scale, blocks_in, count_in, mm, tab, after, pot, atoms, slots, p8, qb, blocks, count, sems):
    copies = fetch((blocks_in, count_in), (blocks, count), sems)
    turned = tab[:, :LANES].T
    x, y, z = (turned[ML_DEV * c : ML_DEV * (c + 1)] for c in range(3))
    p8[...] = jnp.zeros_like(p8)
    for c, value in enumerate((x, y, z, x * x + y * y + z * z, jnp.ones_like(x))):
        p8[pl.ds(c, ML_DEV, stride=8), :] = value

    def atom_tile(t, carry):
        one, two, three = three_parts(p8[pl.ds(pl.multiple_of(t * 8, 8), 8), :])
        atoms[:, pl.ds(pl.multiple_of(t * LANES, LANES), LANES)] = jnp.concatenate(
            [one, one, two, two, one, three], axis=0
        ).astype(jnp.bfloat16)
        return carry

    lax.fori_loop(0, ML_DEV, atom_tile, 0)
    for copy in copies:
        copy.wait()
    nslots = blocks.shape[1]
    for s in range(nslots):
        rows = mm[:, pl.ds(pl.multiple_of(blocks[0, s] * LANES, LANES), LANES)]
        q = rows[3:4] * jnp.where(s < count[0], 1.0, 0.0)
        pos = rows[:3]
        norm = jnp.sum(pos * pos, axis=0, keepdims=True) + 1.0
        eight = jnp.concatenate(
            [-2.0 * pos, jnp.ones_like(q), norm, jnp.zeros((3, LANES), jnp.float32)], axis=0
        )
        one, two, three = three_parts(eight)
        slots[:, s * LANES : (s + 1) * LANES] = jnp.concatenate(
            [one, two, one, two, three, one], axis=0
        ).astype(jnp.bfloat16)
        qb[s * LANES : (s + 1) * LANES, :] = jnp.broadcast_to(q, (LANES, LANES)).T

    def tile(i, carry):
        right = atoms[:, pl.ds(pl.multiple_of(i * 256, 256), 256)]
        total = jnp.zeros((8, 256), jnp.float32)
        for s in range(nslots // 2):
            inv = lax.rsqrt(rows0(slots[:, s * 256 : (s + 1) * 256], right))
            q = qb[s * 256 : (s + 1) * 256, :]
            term = inv * jnp.concatenate([q, q], axis=1)
            total = total + jnp.sum(term.reshape(32, 8, 256), axis=0)
        total = scale * jnp.sum(total, axis=0, keepdims=True)
        pot[pl.ds(2 * i, 1), :] = total[:, :LANES]
        pot[pl.ds(2 * i + 1, 1), :] = total[:, LANES:]
        return carry

    lax.fori_loop(0, ML_DEV // 2, tile, 0, unroll=5)


def field(blocks, count, mm, tab, after, scale):
    nslots = blocks.shape[1]
    hbm = pl.BlockSpec(memory_space=pltpu.HBM)
    vmem = pl.BlockSpec(memory_space=pltpu.VMEM)
    return pl.pallas_call(
        functools.partial(field_kernel, scale),
        out_shape=(
            jax.ShapeDtypeStruct((ML_DEV, LANES), jnp.float32),
            pltpu.HBM((48, ML_DEV * LANES), jnp.bfloat16),
            pltpu.HBM((48, nslots * LANES), jnp.bfloat16),
        ),
        in_specs=[hbm, hbm, vmem, vmem, pl.BlockSpec(memory_space=pl.ANY)],
        out_specs=(vmem,) * 3,
        scratch_shapes=[
            pltpu.VMEM((8 * ML_DEV, LANES), jnp.float32),
            pltpu.VMEM((nslots * LANES, LANES), jnp.float32),
            pltpu.SMEM(blocks.shape, blocks.dtype),
            pltpu.SMEM(count.shape, count.dtype),
            pltpu.SemaphoreType.DMA((2,)),
        ],
        compiler_params=vmem_mib(10),
        name="field",
    )(blocks, count, mm, tab, after)


def lane_iota(shape):
    return lax.broadcasted_iota(jnp.int32, shape, 1)


def exact_pick(left, right):
    left = left.astype(jnp.bfloat16)
    parts = [jnp.dot(left, part.astype(jnp.bfloat16), preferred_element_type=jnp.float32) for part in three_parts(right)]
    return (parts[2] + parts[1]) + parts[0]


def exact_sum(left, right):
    right = right.astype(jnp.bfloat16)
    parts = [jnp.dot(part.astype(jnp.bfloat16), right, preferred_element_type=jnp.float32) for part in three_parts(left)]
    return (parts[2] + parts[1]) + parts[0]


def where_is(me, ids):
    own_ids = me * ML_DEV + jnp.minimum(lax.broadcasted_iota(jnp.int32, (ROWS - EDGES, 1), 0), ML_DEV - 1)
    atom = jnp.concatenate([ids, own_ids], axis=0)
    dev = (atom * 52429) >> 21
    return dev, atom - dev * ML_DEV


def geometry_kernel(me, ids, tab, field_w, charge_w, energy_w, after, basis_out, kinds_out, rows_out, zero):
    zero[...] = jnp.zeros_like(zero)
    rows_out[...] = jnp.concatenate([field_w[...], charge_w[...], energy_w[...], field_w[...]], axis=0)
    dev, t = where_is(me[0], ids[...])
    at_dev = lane_iota((ROWS, LANES)) == dev
    rows = exact_pick(jnp.where(at_dev, 1.0, 0.0), tab[...])
    lane = lane_iota((1, 2 * LANES))
    place = jnp.where(lane < ML_DEV, lane, jnp.where(lane < 2 * ML_DEV, lane - ML_DEV, lane - 2 * ML_DEV))
    place = jnp.where(lane < LANES, place, lane - LANES)
    place = jnp.where(place < ML_DEV, place, -1)
    rows = jnp.where(place == t, rows, 0.0)
    src = lax.broadcasted_iota(jnp.int32, (2 * LANES, LANES), 0)
    dst = lane_iota((2 * LANES, LANES))
    group = jnp.where(src < ML_DEV, 0, jnp.where(src < 2 * ML_DEV, 1, jnp.where(src < LANES, 2, 3)))
    picked = exact_sum(rows, jnp.where(group == dst, 1.0, 0.0))
    own = picked[EDGES : EDGES + ML_DEV]
    centre = jnp.broadcast_to(own[:, None, :], (ML_DEV, KNB, LANES)).reshape(EDGES, LANES)
    gap = picked[:EDGES] - centre
    lanes = lane_iota((EDGES, LANES))
    dist = jnp.sqrt(exact_sum(jnp.where(lanes < 3, gap * gap, 0.0), jnp.ones((LANES, LANES), jnp.float32)))
    shift = dist - 0.5 * (lanes & 7).astype(jnp.float32)
    one, two, three = three_parts(jnp.exp(-2.0 * (shift * shift)))
    part = lanes >> 3
    value = jnp.where((part < 2) | (part == 4), one, jnp.where(part < 4, two, three))
    basis_out[...] = jnp.where(part < 6, value, 0.0).astype(jnp.bfloat16)
    kind = jnp.broadcast_to(picked[:, 3:4], (ROWS, LANES)).astype(jnp.int32)
    lanes = lane_iota((ROWS, LANES))
    kinds_out[...] = jnp.where((kind == (lanes & 15)) & (lanes < 48), 1.0, 0.0).astype(jnp.bfloat16)


def geometry(me, ids, tab, field_w, charge_w, energy_w, after):
    smem = pl.BlockSpec(memory_space=pltpu.SMEM)
    vmem = pl.BlockSpec(memory_space=pltpu.VMEM)
    return pl.pallas_call(
        geometry_kernel,
        out_shape=(
            jax.ShapeDtypeStruct((EDGES, LANES), jnp.bfloat16),
            jax.ShapeDtypeStruct((ROWS, LANES), jnp.bfloat16),
            jax.ShapeDtypeStruct((4, field_w.shape[1]), jnp.float32),
            jax.ShapeDtypeStruct((1, LANES), jnp.float32),
        ),
        in_specs=[smem] + [vmem] * 5 + [pl.BlockSpec(memory_space=pl.ANY)],
        out_specs=(vmem,) * 4,
        compiler_params=vmem_mib(20),
        name="geometry",
    )(me, ids, tab, field_w, charge_w, energy_w, after)


def radial_of(basis, weights):
    one, two, three = three_parts(weights)
    rest = jnp.zeros((LANES - 48, weights.shape[1]), jnp.float32)
    stacked = jnp.concatenate([one, two, one, two, three, one, rest], axis=0).astype(jnp.bfloat16)
    return jnp.dot(basis, stacked, preferred_element_type=jnp.float32)


def first_layer_kernel(
    me, ids, pot, basis, kinds, table, field_w, msg, radial_w, mix, feat_out, proj_out
):
    pot_rows = jnp.concatenate([pot[...], jnp.zeros((LANES - ML_DEV, LANES), jnp.float32)], axis=0).T
    dev, t = where_is(me[0], ids[...])
    lanes = lane_iota((ROWS, LANES))
    rows = exact_pick(jnp.where(lanes == dev, 1.0, 0.0), pot_rows)
    pot_of = jnp.sum(jnp.where(lanes == t, rows, 0.0), axis=1, keepdims=True)
    channels = msg.shape[1]
    lines = jnp.concatenate([table[...], jnp.zeros((16 - table.shape[0], channels), jnp.float32)], axis=0)
    lines = jnp.concatenate(three_parts(lines) + (jnp.zeros((LANES - 48, channels), jnp.float32),), axis=0)
    feat = jnp.dot(kinds[...], lines.astype(jnp.bfloat16), preferred_element_type=jnp.float32)
    feat = feat + pot_of * field_w[:1]
    proj = jnp.dot(feat[:EDGES].astype(jnp.bfloat16), msg[0], preferred_element_type=jnp.float32)
    proj = proj.astype(jnp.bfloat16).astype(jnp.float32)
    radial = radial_of(basis[...], radial_w[0])
    message = jnp.sum((radial * proj).reshape(ML_DEV, KNB, channels), axis=1) * (1.0 / KNB)
    update = jnp.dot(message.astype(jnp.bfloat16), mix[0], preferred_element_type=jnp.float32)
    feat1 = feat[EDGES : EDGES + ML_DEV] + update * lax.logistic(update)
    feat_out[:, :channels] = feat1
    feat_out[:, channels:] = jnp.broadcast_to(pot_of[EDGES : EDGES + ML_DEV], (ML_DEV, LANES))
    proj_out[...] = jnp.dot(feat1.astype(jnp.bfloat16), msg[1], preferred_element_type=jnp.float32).astype(jnp.bfloat16)


def first_layer(*args):
    channels = args[7].shape[1]
    smem = pl.BlockSpec(memory_space=pltpu.SMEM)
    vmem = pl.BlockSpec(memory_space=pltpu.VMEM)
    return pl.pallas_call(
        first_layer_kernel,
        out_shape=(
            jax.ShapeDtypeStruct((ML_DEV, channels + LANES), jnp.float32),
            jax.ShapeDtypeStruct((ML_DEV, channels), jnp.bfloat16),
        ),
        in_specs=[smem] + [vmem] * 9,
        out_specs=(vmem,) * 2,
        compiler_params=vmem_mib(20),
        name="first_layer",
    )(*args)


def fetch(sources, places, sems):
    copies = [pltpu.make_async_copy(src, dst, sems.at[i]) for i, (src, dst) in enumerate(zip(sources, places))]
    for copy in copies:
        copy.start()
    return copies


def second_layer_kernel(
    me, ids_in, basis_in, feat1, radial_in, mix_in, rows_in, p0, p1, p2, p3, p4, p5, p6, p7,
    charge_out, energy_out, proj, ids, basis, feat_v, radial_w, mix, lines, sems,
):
    parts = (p0, p1, p2, p3, p4, p5, p6, p7)
    size = p0.shape[0]
    copies = fetch(
        (ids_in, basis_in, feat1, radial_in, mix_in, rows_in) + parts,
        [ids, basis, feat_v, radial_w, mix, lines]
        + [proj.at[pl.ds(i * size, size)] for i in range(8)],
        sems,
    )
    copies[0].wait()
    part = 256
    mine = me[0]
    messages = []
    for m in range(EDGES // part):
        here = slice(m * part, (m + 1) * part)
        atom = ids[here, :]
        dev = (atom * 52429) >> 21
        t = atom - dev * ML_DEV
        far_c = (mine ^ dev) & 1
        far_z = ((mine >> 2) - (dev >> 2)) & 3
        far_x = ((mine >> 5) - (dev >> 5)) & 3
        row_of = lambda v: 2 * ((v >> 4) & 1) + ((v >> 1) & 1)
        far_y = (row_of(mine) - row_of(dev)) & 3
        odd = (dev & 1) == 1
        far = (far_x, far_y, far_z)
        k1, k2, k3 = (jnp.where(odd, far[STAGES[1][i]], far[STAGES[0][i]]) for i in range(3))
        place = ((far_c * 4 + k3) * 16 + k2 * 4 + k1) * ML_DEV + t
        same = lane_iota((part, 8 * size)).astype(jnp.int16) == place.astype(jnp.int16)
        pick = jnp.where(same, jnp.bfloat16(1), jnp.bfloat16(0))
        if m == 0:
            for copy in copies[1:]:
                copy.wait()
        rows = jnp.dot(pick, proj[...], preferred_element_type=jnp.float32)
        radial = radial_of(basis[here, :], radial_w[1])
        messages.append(jnp.sum((radial * rows).reshape(part // KNB, KNB, rows.shape[1]), axis=1) * (1.0 / KNB))
    message = jnp.concatenate(messages, axis=0).astype(jnp.bfloat16)
    update = jnp.dot(message, mix[1], preferred_element_type=jnp.float32)
    channels = update.shape[1]
    feat = feat_v[:, :channels] + update * lax.logistic(update)
    charge = jnp.tanh(jnp.sum(feat * lines[1:2], axis=1, keepdims=True))
    energy = jnp.sum(feat * lines[2:3], axis=1, keepdims=True) + charge * feat_v[:, channels : channels + 1]

    def as_row(column):
        square = jnp.broadcast_to(column, (ML_DEV, LANES))
        return jnp.concatenate([square, jnp.zeros((LANES - ML_DEV, LANES), jnp.float32)], axis=0).T

    charge_out[...] = as_row(charge)
    energy_out[...] = as_row(energy)[:1]


def second_layer(*args):
    smem = pl.BlockSpec(memory_space=pltpu.SMEM)
    vmem = pl.BlockSpec(memory_space=pltpu.VMEM)
    like = lambda a: pltpu.VMEM(a.shape, a.dtype)
    parts = args[7:]
    rows, channels = parts[0].shape
    return pl.pallas_call(
        second_layer_kernel,
        out_shape=(
            jax.ShapeDtypeStruct((NDEV, LANES), jnp.float32),
            pltpu.HBM((1, LANES), jnp.float32),
        ),
        in_specs=[smem] + [pl.BlockSpec(memory_space=pltpu.HBM)] * 14,
        out_specs=(vmem,) * 2,
        scratch_shapes=[pltpu.VMEM((8 * rows, channels), jnp.bfloat16)]
        + [like(a) for a in args[1:7]]
        + [pltpu.SemaphoreType.DMA((14,))],
        compiler_params=vmem_mib(24),
        name="second_layer",
    )(*args)


def embed_kernel(scale, mm, tab, charges, blocks_in, count_in, atoms_in, slots_in, *rest):
    pieces, (out, c8, left, total, blocks, count, atoms, slots, sems) = rest[:-9], rest[-9:]
    begins = [sum(piece.shape[1] for piece in pieces[:i]) for i in range(len(pieces))]
    copies = fetch(
        (atoms_in, slots_in, blocks_in, count_in) + pieces,
        [atoms, slots, blocks, count]
        + [out.at[:, pl.ds(begin, piece.shape[1])] for begin, piece in zip(begins, pieces)],
        sems,
    )
    turned = tab[:, :LANES].T
    charge = charges[...].T[:ML_DEV]
    c8[...] = jnp.zeros_like(c8)
    c8[pl.ds(0, ML_DEV, stride=8), :] = charge
    for c in range(3):
        c8[pl.ds(c + 1, ML_DEV, stride=8), :] = charge * turned[ML_DEV * c : ML_DEV * (c + 1)]

    def charge_tile(t, carry):
        one, two, _ = three_parts(c8[pl.ds(pl.multiple_of(t * 8, 8), 8), :])
        left[:, pl.ds(pl.multiple_of(t * LANES, LANES), LANES)] = jnp.concatenate([one, two], axis=0).astype(
            jnp.bfloat16
        )
        return carry

    lax.fori_loop(0, ML_DEV, charge_tile, 0)
    nslots = blocks.shape[1]
    total[...] = jnp.zeros_like(total)
    copies[0].wait()
    copies[1].wait()

    def tile(i, carry):
        cols = pl.ds(pl.multiple_of(i * 256, 256), 256)
        some = atoms[:, cols]
        lhs = left[:, cols]
        for s in range(nslots // 2):
            inv = lax.rsqrt(rows0(some, slots[:, s * 256 : (s + 1) * 256]))
            cube = inv * inv * inv
            high = cube.astype(jnp.bfloat16)
            low = (cube - high.astype(jnp.float32)).astype(jnp.bfloat16)
            total[:, s * 256 : (s + 1) * 256] += jnp.dot(lhs, high, preferred_element_type=jnp.float32) + jnp.dot(
                lhs, low, preferred_element_type=jnp.float32
            )
        return carry

    lax.fori_loop(0, ML_DEV // 2, tile, 0, unroll=10)
    for copy in copies[2:]:
        copy.wait()
    for s in range(nslots):
        here = pl.ds(pl.multiple_of(blocks[0, s] * LANES, LANES), LANES)
        rows = mm[:, here]
        q = rows[3:4] * (scale * jnp.where(s < count[0], 1.0, 0.0))
        sums = total[:, s * LANES : (s + 1) * LANES]
        sums = sums[:8] + sums[8:]
        out[:, here] += q * (rows[:3] * sums[0:1] - sums[1:4])


def embed(blocks, count, mm, tab, charges, atoms, slots, pieces, scale):
    vmem = pl.BlockSpec(memory_space=pltpu.VMEM)
    return pl.pallas_call(
        functools.partial(embed_kernel, scale),
        out_shape=jax.ShapeDtypeStruct((3, mm.shape[1]), jnp.float32),
        in_specs=[vmem] * 3 + [pl.BlockSpec(memory_space=pltpu.HBM)] * (4 + len(pieces)),
        out_specs=vmem,
        scratch_shapes=[
            pltpu.VMEM((8 * ML_DEV, LANES), jnp.float32),
            pltpu.VMEM((16, ML_DEV * LANES), jnp.bfloat16),
            pltpu.VMEM((16, slots.shape[1]), jnp.float32),
            pltpu.SMEM(blocks.shape, blocks.dtype),
            pltpu.SMEM(count.shape, count.dtype),
            pltpu.VMEM(atoms.shape, atoms.dtype),
            pltpu.VMEM(slots.shape, slots.dtype),
            pltpu.SemaphoreType.DMA((4 + len(pieces),)),
        ],
        compiler_params=vmem_mib(12),
        name="embed_forces",
    )(mm, tab, charges, blocks, count, atoms, slots, *pieces)


def stage_parts(value, stage):
    parts = [value]
    for k in range(1, 4):
        pairs = []
        for dev in range(NDEV):
            at = [dev >> 5, 2 * ((dev >> 4) & 1) + ((dev >> 1) & 1), (dev >> 2) & 3]
            axis = STAGES[dev & 1][stage]
            at[axis] = (at[axis] + k) % 4
            x, y, z = at
            pairs.append((dev, (x << 5) + ((y >> 1) << 4) + (z << 2) + ((y & 1) << 1) + (dev & 1)))
        parts.append(lax.ppermute(value, ALL, pairs))
    return parts


def ring_parts(value, axis):
    n = lax.axis_size(axis)
    return [value] + [lax.ppermute(value, axis, [(i, (i + k) % n) for i in range(n)]) for k in range(1, n)]


def stand(value, zero):
    return value + zero[:, : value.shape[1]].astype(value.dtype)


def body(
    mm_atoms,
    neighbours,
    embed_blocks,
    embed_count,
    ml_coords,
    ml_species,
    ml_edges,
    species_table,
    field_weight,
    msg_weight,
    radial_weight,
    mix_weight,
    charge_weight,
    energy_weight,
):
    own_rows = mm_atoms.shape[1]
    kappa = 4.0 / math.sqrt(NDEV * ML_DEV)
    kappa_field = 3.0 / math.sqrt(NDEV * embed_blocks.shape[1] * LANES)
    me = lax.axis_index(ALL)[None]
    tab = lax.all_to_all(spread(ml_coords, ml_species[None]), ALL, 0, 0, tiled=True)
    tab = tab.reshape(NDEV, 2 * LANES)
    ids = ml_edges.reshape(-1, 1)
    blocks = own_rows // LANES
    cuts = (0, 12, 44, 52, 60, 76, 100, blocks - 12, blocks)
    far = ml_coords

    def pairs(i, *after, before=far, behind=far):
        return pair_forces(cuts[i], cuts[i + 1] - cuts[i], before, mm_atoms, behind, neighbours, after)

    pieces = [None] * (len(cuts) - 1)
    pieces[1], zero = pairs(1, embed_blocks, radial_weight)
    pot, atoms, slots = field(embed_blocks, embed_count, mm_atoms, tab, pieces[1], kappa_field)
    basis, kinds, rows, zero = geometry(
        me, ids, tab, field_weight[None], charge_weight[None], energy_weight[None], pot
    )
    pot = functools.reduce(jnp.add, ring_parts(pot, "c"))
    pot = stand(functools.reduce(jnp.add, stage_parts(pot, 0)), zero)
    pot = functools.reduce(jnp.add, stage_parts(pot, 1))
    pieces[2], zero = pairs(2, pot)
    pot = stand(functools.reduce(jnp.add, stage_parts(pot, 2)), zero)
    feat1, proj = first_layer(
        me, ids, pot, basis, kinds, species_table, rows, msg_weight, radial_weight, mix_weight
    )
    for i, stage in ((3, 0), (4, 1)):
        pieces[i], zero = pairs(i, proj)
        proj = stand(jnp.concatenate(stage_parts(proj, stage), axis=0), zero)
    halo = HALO_BLOCKS * LANES
    up = [(i, (i + 1) % NDEV) for i in range(NDEV)]
    down = [(j, i) for i, j in up]
    before = lax.ppermute(stand(mm_atoms[:, own_rows - halo :], zero), ALL, up)
    behind = lax.ppermute(stand(mm_atoms[:, :halo], zero), ALL, down)
    pieces[5], zero = pairs(5, proj)
    parts = stage_parts(proj, 2)
    parts[1:] = [stand(part, zero) for part in parts[1:]]
    parts = parts + [ring_parts(part, "c")[1] for part in parts]
    charges, energy = second_layer(
        me,
        ids,
        basis,
        feat1,
        radial_weight,
        mix_weight,
        rows,
        *parts,
    )
    pieces[6], _ = pairs(6, charges)
    for i in (0, 7):
        pieces[i], _ = pairs(i, charges, before=before, behind=behind)
    charges = lax.all_to_all(charges, ALL, 0, 0, tiled=True)
    mm_force = embed(embed_blocks, embed_count, mm_atoms, tab, charges, atoms, slots, pieces, kappa)
    return (energy[0, :ML_DEV], mm_force)


def solution(mesh):
    fine = Mesh(mesh.devices.reshape(4, 2, 4, 2, 2), ALL)
    in_specs = (
        P(None, ALL),
        P(None, ALL),
        P(ALL, None),
        P(ALL),
        P(None, ALL),
        P(ALL),
        P(ALL, None),
        P(),
        P(),
        P(),
        P(),
        P(),
        P(),
        P(),
    )
    out_specs = (P(ALL), P(None, ALL))
    return jax.shard_map(body, mesh=fine, in_specs=in_specs, out_specs=out_specs, check_vma=False)
```

```python
import functools
import math

import jax
import jax.numpy as jnp
from jax import lax
from jax.experimental import pallas as pl
from jax.experimental.pallas import tpu as pltpu
from jax.sharding import Mesh
from jax.sharding import PartitionSpec as P

ALL = ("x", "yh", "z", "yl", "c")
STAGES = ((2, 0, 1), (0, 1, 2))
vmem_mib = lambda size: pltpu.CompilerParams(vmem_limit_bytes=size * 1024 * 1024)
LANES = 128
NDEV = 128
ML_DEV = 40
KNB = 32
EDGES = ML_DEV * KNB
ROWS = 1344
HALO_BLOCKS = 8
PAIR_STEP = 4


def rows0(left, right):
    return lax.dot_general(
        left, right, (((0,), (0,)), ((), ())), preferred_element_type=jnp.float32
    )


def pair_kernel(first, count, left, own, right, nb, *rest):
    out, zero, ext = rest[-3:]
    own_blocks = own.shape[1] // LANES
    step = pl.program_id(0)

    @pl.when(step == 0)
    def _():
        zero[...] = jnp.zeros_like(zero)
        low, high = first - HALO_BLOCKS, first + count + HALO_BLOCKS
        for src, begin, size in ((left, -HALO_BLOCKS, HALO_BLOCKS), (own, 0, own_blocks), (right, own_blocks, HALO_BLOCKS)):
            start, stop = max(low, begin), min(high, begin + size)
            if start >= stop:
                continue

            def fill(r, carry, src=src, begin=begin):
                rows = src[:, pl.ds(pl.multiple_of((r - begin) * LANES, LANES), LANES)]
                for c in range(4):
                    ext[c, r - low] = jnp.broadcast_to(rows[c : c + 1], (8, LANES))
                return carry

            lax.fori_loop(start, stop, fill, 0)

    blocks = nb.shape[1] // LANES

    def block(j, carry):
        b = step * blocks + j
        lanes = pl.ds(pl.multiple_of(j * LANES, LANES), LANES)
        rel = nb[:, lanes] - (b + first) * LANES
        row = rel >> 7
        lane = rel & 127
        centre = [ext[c, b + HALO_BLOCKS] for c in range(4)]
        total = [jnp.zeros((8, LANES), jnp.float32) for _ in range(3)]
        for h in range(nb.shape[0] // 8):
            near = row[8 * h : 8 * h + 8]
            pick = lane[8 * h : 8 * h + 8]
            got = [jnp.zeros((8, LANES), jnp.float32) for _ in range(4)]
            for k in range(2 * HALO_BLOCKS + 1):
                here = near == k
                for c in range(4):
                    value = jnp.take_along_axis(ext[c, b + k], pick, axis=1, mode="promise_in_bounds")
                    got[c] = jnp.where(here, value, got[c])
            off = [centre[c] - got[c] for c in range(3)]
            inv = lax.rsqrt(off[0] * off[0] + off[1] * off[1] + off[2] * off[2] + 1.0)
            strength = centre[3] * got[3] * (inv * inv * inv)
            for c in range(3):
                total[c] = total[c] + strength * off[c]
        for c in range(3):
            out[c : c + 1, lanes] = jnp.sum(total[c], axis=0, keepdims=True)
        return carry

    lax.fori_loop(0, blocks, block, 0, unroll=PAIR_STEP)


def pair_forces(first, count, left, own, right, neighbours, after):
    wide = PAIR_STEP * LANES
    whole = lambda a: pl.BlockSpec(a.shape, lambda i: (0, 0))
    slots = neighbours.shape[0]
    return pl.pallas_call(
        functools.partial(pair_kernel, first, count),
        grid=(count // PAIR_STEP,),
        out_shape=(
            jax.ShapeDtypeStruct((3, count * LANES), jnp.float32),
            jax.ShapeDtypeStruct((1, HALO_BLOCKS * LANES), jnp.float32),
        ),
        in_specs=[
            whole(left),
            whole(own),
            whole(right),
            pl.BlockSpec((slots, wide), lambda i: (0, i + first // PAIR_STEP)),
            *[pl.BlockSpec(memory_space=pl.ANY)] * len(after),
        ],
        out_specs=(
            pl.BlockSpec((3, wide), lambda i: (0, i)),
            pl.BlockSpec((1, HALO_BLOCKS * LANES), lambda i: (0, 0)),
        ),
        scratch_shapes=[pltpu.VMEM((4, count + 2 * HALO_BLOCKS, 8, LANES), jnp.float32)],
        compiler_params=vmem_mib(6),
        cost_estimate=pl.CostEstimate(
            flops=count * 10**7, bytes_accessed=count * 16384, transcendentals=count * slots * LANES
        ),
        name="pair_forces",
    )(left, own, right, neighbours, *after)


def spread_kernel(coords, species, out):
    rows = [coords[c : c + 1, :] for c in range(3)] + [species[...].astype(jnp.float32)]
    rows = rows[:3] + [jnp.zeros((1, 8), jnp.float32)] + rows[3:] + [jnp.zeros((1, LANES - ML_DEV), jnp.float32)]
    out[:, 0, :] = jnp.broadcast_to(jnp.concatenate(rows, axis=1), (NDEV, 2 * LANES))


def spread(coords, species):
    vmem = pl.BlockSpec(memory_space=pltpu.VMEM)
    return pl.pallas_call(
        spread_kernel,
        out_shape=jax.ShapeDtypeStruct((NDEV, 1, 2 * LANES), jnp.float32),
        in_specs=[vmem, vmem],
        out_specs=vmem,
        name="spread",
    )(coords, species)


def three_parts(value):
    one = value.astype(jnp.bfloat16).astype(jnp.float32)
    rest = value - one
    two = rest.astype(jnp.bfloat16).astype(jnp.float32)
    three = (rest - two).astype(jnp.bfloat16).astype(jnp.float32)
    return one, two, three


def field_kernel(scale, blocks_in, count_in, mm, tab, after, pot, atoms, slots, p8, qb, blocks, count, sems):
    copies = fetch((blocks_in, count_in), (blocks, count), sems)
    turned = tab[:, :LANES].T
    x, y, z = (turned[ML_DEV * c : ML_DEV * (c + 1)] for c in range(3))
    p8[...] = jnp.zeros_like(p8)
    for c, value in enumerate((x, y, z, x * x + y * y + z * z, jnp.ones_like(x))):
        p8[pl.ds(c, ML_DEV, stride=8), :] = value

    def atom_tile(t, carry):
        one, two, three = three_parts(p8[pl.ds(pl.multiple_of(t * 8, 8), 8), :])
        atoms[:, pl.ds(pl.multiple_of(t * LANES, LANES), LANES)] = jnp.concatenate(
            [one, one, two, two, one, three], axis=0
        ).astype(jnp.bfloat16)
        return carry

    lax.fori_loop(0, ML_DEV, atom_tile, 0)
    for copy in copies:
        copy.wait()
    nslots = blocks.shape[1]
    for s in range(nslots):
        rows = mm[:, pl.ds(pl.multiple_of(blocks[0, s] * LANES, LANES), LANES)]
        q = rows[3:4] * jnp.where(s < count[0], 1.0, 0.0)
        pos = rows[:3]
        norm = jnp.sum(pos * pos, axis=0, keepdims=True) + 1.0
        eight = jnp.concatenate(
            [-2.0 * pos, jnp.ones_like(q), norm, jnp.zeros((3, LANES), jnp.float32)], axis=0
        )
        one, two, three = three_parts(eight)
        slots[:, s * LANES : (s + 1) * LANES] = jnp.concatenate(
            [one, two, one, two, three, one], axis=0
        ).astype(jnp.bfloat16)
        qb[s * LANES : (s + 1) * LANES, :] = jnp.broadcast_to(q, (LANES, LANES)).T

    def tile(i, carry):
        right = atoms[:, pl.ds(pl.multiple_of(i * 256, 256), 256)]
        total = jnp.zeros((8, 256), jnp.float32)
        for s in range(nslots // 2):
            inv = lax.rsqrt(rows0(slots[:, s * 256 : (s + 1) * 256], right))
            q = qb[s * 256 : (s + 1) * 256, :]
            term = inv * jnp.concatenate([q, q], axis=1)
            total = total + jnp.sum(term.reshape(32, 8, 256), axis=0)
        total = scale * jnp.sum(total, axis=0, keepdims=True)
        pot[pl.ds(2 * i, 1), :] = total[:, :LANES]
        pot[pl.ds(2 * i + 1, 1), :] = total[:, LANES:]
        return carry

    lax.fori_loop(0, ML_DEV // 2, tile, 0, unroll=5)


def field(blocks, count, mm, tab, after, scale):
    nslots = blocks.shape[1]
    hbm = pl.BlockSpec(memory_space=pltpu.HBM)
    vmem = pl.BlockSpec(memory_space=pltpu.VMEM)
    return pl.pallas_call(
        functools.partial(field_kernel, scale),
        out_shape=(
            jax.ShapeDtypeStruct((ML_DEV, LANES), jnp.float32),
            pltpu.HBM((48, ML_DEV * LANES), jnp.bfloat16),
            pltpu.HBM((48, nslots * LANES), jnp.bfloat16),
        ),
        in_specs=[hbm, hbm, vmem, vmem, pl.BlockSpec(memory_space=pl.ANY)],
        out_specs=(vmem,) * 3,
        scratch_shapes=[
            pltpu.VMEM((8 * ML_DEV, LANES), jnp.float32),
            pltpu.VMEM((nslots * LANES, LANES), jnp.float32),
            pltpu.SMEM(blocks.shape, blocks.dtype),
            pltpu.SMEM(count.shape, count.dtype),
            pltpu.SemaphoreType.DMA((2,)),
        ],
        compiler_params=vmem_mib(10),
        name="field",
    )(blocks, count, mm, tab, after)


def lane_iota(shape):
    return lax.broadcasted_iota(jnp.int32, shape, 1)


def exact_pick(left, right):
    left = left.astype(jnp.bfloat16)
    parts = [jnp.dot(left, part.astype(jnp.bfloat16), preferred_element_type=jnp.float32) for part in three_parts(right)]
    return (parts[2] + parts[1]) + parts[0]


def exact_sum(left, right):
    right = right.astype(jnp.bfloat16)
    parts = [jnp.dot(part.astype(jnp.bfloat16), right, preferred_element_type=jnp.float32) for part in three_parts(left)]
    return (parts[2] + parts[1]) + parts[0]


def where_is(me, ids):
    own_ids = me * ML_DEV + jnp.minimum(lax.broadcasted_iota(jnp.int32, (ROWS - EDGES, 1), 0), ML_DEV - 1)
    atom = jnp.concatenate([ids, own_ids], axis=0)
    dev = (atom * 52429) >> 21
    return dev, atom - dev * ML_DEV


def geometry_kernel(me, ids, tab, field_w, charge_w, energy_w, after, basis_out, kinds_out, rows_out, zero):
    zero[...] = jnp.zeros_like(zero)
    rows_out[...] = jnp.concatenate([field_w[...], charge_w[...], energy_w[...], field_w[...]], axis=0)
    dev, t = where_is(me[0], ids[...])
    at_dev = lane_iota((ROWS, LANES)) == dev
    rows = exact_pick(jnp.where(at_dev, 1.0, 0.0), tab[...])
    lane = lane_iota((1, 2 * LANES))
    place = jnp.where(lane < ML_DEV, lane, jnp.where(lane < 2 * ML_DEV, lane - ML_DEV, lane - 2 * ML_DEV))
    place = jnp.where(lane < LANES, place, lane - LANES)
    place = jnp.where(place < ML_DEV, place, -1)
    rows = jnp.where(place == t, rows, 0.0)
    src = lax.broadcasted_iota(jnp.int32, (2 * LANES, LANES), 0)
    dst = lane_iota((2 * LANES, LANES))
    group = jnp.where(src < ML_DEV, 0, jnp.where(src < 2 * ML_DEV, 1, jnp.where(src < LANES, 2, 3)))
    picked = exact_sum(rows, jnp.where(group == dst, 1.0, 0.0))
    own = picked[EDGES : EDGES + ML_DEV]
    centre = jnp.broadcast_to(own[:, None, :], (ML_DEV, KNB, LANES)).reshape(EDGES, LANES)
    gap = picked[:EDGES] - centre
    lanes = lane_iota((EDGES, LANES))
    dist = jnp.sqrt(exact_sum(jnp.where(lanes < 3, gap * gap, 0.0), jnp.ones((LANES, LANES), jnp.float32)))
    shift = dist - 0.5 * (lanes & 7).astype(jnp.float32)
    one, two, three = three_parts(jnp.exp(-2.0 * (shift * shift)))
    part = lanes >> 3
    value = jnp.where((part < 2) | (part == 4), one, jnp.where(part < 4, two, three))
    basis_out[...] = jnp.where(part < 6, value, 0.0).astype(jnp.bfloat16)
    kind = jnp.broadcast_to(picked[:, 3:4], (ROWS, LANES)).astype(jnp.int32)
    lanes = lane_iota((ROWS, LANES))
    kinds_out[...] = jnp.where((kind == (lanes & 15)) & (lanes < 48), 1.0, 0.0).astype(jnp.bfloat16)


def geometry(me, ids, tab, field_w, charge_w, energy_w, after):
    smem = pl.BlockSpec(memory_space=pltpu.SMEM)
    vmem = pl.BlockSpec(memory_space=pltpu.VMEM)
    return pl.pallas_call(
        geometry_kernel,
        out_shape=(
            jax.ShapeDtypeStruct((EDGES, LANES), jnp.bfloat16),
            jax.ShapeDtypeStruct((ROWS, LANES), jnp.bfloat16),
            jax.ShapeDtypeStruct((4, field_w.shape[1]), jnp.float32),
            jax.ShapeDtypeStruct((1, LANES), jnp.float32),
        ),
        in_specs=[smem] + [vmem] * 5 + [pl.BlockSpec(memory_space=pl.ANY)],
        out_specs=(vmem,) * 4,
        compiler_params=vmem_mib(20),
        name="geometry",
    )(me, ids, tab, field_w, charge_w, energy_w, after)


def radial_of(basis, weights):
    one, two, three = three_parts(weights)
    rest = jnp.zeros((LANES - 48, weights.shape[1]), jnp.float32)
    stacked = jnp.concatenate([one, two, one, two, three, one, rest], axis=0).astype(jnp.bfloat16)
    return jnp.dot(basis, stacked, preferred_element_type=jnp.float32)


def first_layer_kernel(
    me, ids, pot, basis, kinds, table, field_w, msg, radial_w, mix, feat_out, proj_out
):
    pot_rows = jnp.concatenate([pot[...], jnp.zeros((LANES - ML_DEV, LANES), jnp.float32)], axis=0).T
    dev, t = where_is(me[0], ids[...])
    lanes = lane_iota((ROWS, LANES))
    rows = exact_pick(jnp.where(lanes == dev, 1.0, 0.0), pot_rows)
    pot_of = jnp.sum(jnp.where(lanes == t, rows, 0.0), axis=1, keepdims=True)
    channels = msg.shape[1]
    lines = jnp.concatenate([table[...], jnp.zeros((16 - table.shape[0], channels), jnp.float32)], axis=0)
    lines = jnp.concatenate(three_parts(lines) + (jnp.zeros((LANES - 48, channels), jnp.float32),), axis=0)
    feat = jnp.dot(kinds[...], lines.astype(jnp.bfloat16), preferred_element_type=jnp.float32)
    feat = feat + pot_of * field_w[:1]
    proj = jnp.dot(feat[:EDGES].astype(jnp.bfloat16), msg[0], preferred_element_type=jnp.float32)
    proj = proj.astype(jnp.bfloat16).astype(jnp.float32)
    radial = radial_of(basis[...], radial_w[0])
    message = jnp.sum((radial * proj).reshape(ML_DEV, KNB, channels), axis=1) * (1.0 / KNB)
    update = jnp.dot(message.astype(jnp.bfloat16), mix[0], preferred_element_type=jnp.float32)
    feat1 = feat[EDGES : EDGES + ML_DEV] + update * lax.logistic(update)
    feat_out[:, :channels] = feat1
    feat_out[:, channels:] = jnp.broadcast_to(pot_of[EDGES : EDGES + ML_DEV], (ML_DEV, LANES))
    proj_out[...] = jnp.dot(feat1.astype(jnp.bfloat16), msg[1], preferred_element_type=jnp.float32).astype(jnp.bfloat16)


def first_layer(*args):
    channels = args[7].shape[1]
    smem = pl.BlockSpec(memory_space=pltpu.SMEM)
    vmem = pl.BlockSpec(memory_space=pltpu.VMEM)
    return pl.pallas_call(
        first_layer_kernel,
        out_shape=(
            jax.ShapeDtypeStruct((ML_DEV, channels + LANES), jnp.float32),
            jax.ShapeDtypeStruct((ML_DEV, channels), jnp.bfloat16),
        ),
        in_specs=[smem] + [vmem] * 9,
        out_specs=(vmem,) * 2,
        compiler_params=vmem_mib(20),
        name="first_layer",
    )(*args)


def fetch(sources, places, sems):
    copies = [pltpu.make_async_copy(src, dst, sems.at[i]) for i, (src, dst) in enumerate(zip(sources, places))]
    for copy in copies:
        copy.start()
    return copies


def second_layer_kernel(
    me, ids_in, basis_in, feat1, radial_in, mix_in, rows_in, p0, p1, p2, p3, p4, p5, p6, p7,
    charge_out, energy_out, proj, ids, basis, feat_v, radial_w, mix, lines, sems,
):
    parts = (p0, p1, p2, p3, p4, p5, p6, p7)
    size = p0.shape[0]
    copies = fetch(
        (ids_in, basis_in, feat1, radial_in, mix_in, rows_in) + parts,
        [ids, basis, feat_v, radial_w, mix, lines]
        + [proj.at[pl.ds(i * size, size)] for i in range(8)],
        sems,
    )
    copies[0].wait()
    part = 256
    mine = me[0]
    messages = []
    for m in range(EDGES // part):
        here = slice(m * part, (m + 1) * part)
        atom = ids[here, :]
        dev = (atom * 52429) >> 21
        t = atom - dev * ML_DEV
        far_c = (mine ^ dev) & 1
        far_z = ((mine >> 2) - (dev >> 2)) & 3
        far_x = ((mine >> 5) - (dev >> 5)) & 3
        row_of = lambda v: 2 * ((v >> 4) & 1) + ((v >> 1) & 1)
        far_y = (row_of(mine) - row_of(dev)) & 3
        odd = (dev & 1) == 1
        far = (far_x, far_y, far_z)
        k1, k2, k3 = (jnp.where(odd, far[STAGES[1][i]], far[STAGES[0][i]]) for i in range(3))
        place = ((far_c * 4 + k3) * 16 + k2 * 4 + k1) * ML_DEV + t
        same = lane_iota((part, 8 * size)).astype(jnp.int16) == place.astype(jnp.int16)
        pick = jnp.where(same, jnp.bfloat16(1), jnp.bfloat16(0))
        if m == 0:
            for copy in copies[1:]:
                copy.wait()
        rows = jnp.dot(pick, proj[...], preferred_element_type=jnp.float32)
        radial = radial_of(basis[here, :], radial_w[1])
        messages.append(jnp.sum((radial * rows).reshape(part // KNB, KNB, rows.shape[1]), axis=1) * (1.0 / KNB))
    message = jnp.concatenate(messages, axis=0).astype(jnp.bfloat16)
    update = jnp.dot(message, mix[1], preferred_element_type=jnp.float32)
    channels = update.shape[1]
    feat = feat_v[:, :channels] + update * lax.logistic(update)
    charge = jnp.tanh(jnp.sum(feat * lines[1:2], axis=1, keepdims=True))
    energy = jnp.sum(feat * lines[2:3], axis=1, keepdims=True) + charge * feat_v[:, channels : channels + 1]

    def as_row(column):
        square = jnp.broadcast_to(column, (ML_DEV, LANES))
        return jnp.concatenate([square, jnp.zeros((LANES - ML_DEV, LANES), jnp.float32)], axis=0).T

    charge_out[...] = as_row(charge)
    energy_out[...] = as_row(energy)[:1]


def second_layer(*args):
    smem = pl.BlockSpec(memory_space=pltpu.SMEM)
    vmem = pl.BlockSpec(memory_space=pltpu.VMEM)
    like = lambda a: pltpu.VMEM(a.shape, a.dtype)
    parts = args[7:]
    rows, channels = parts[0].shape
    return pl.pallas_call(
        second_layer_kernel,
        out_shape=(
            jax.ShapeDtypeStruct((NDEV, LANES), jnp.float32),
            pltpu.HBM((1, LANES), jnp.float32),
        ),
        in_specs=[smem] + [pl.BlockSpec(memory_space=pltpu.HBM)] * 14,
        out_specs=(vmem,) * 2,
        scratch_shapes=[pltpu.VMEM((8 * rows, channels), jnp.bfloat16)]
        + [like(a) for a in args[1:7]]
        + [pltpu.SemaphoreType.DMA((14,))],
        compiler_params=vmem_mib(24),
        name="second_layer",
    )(*args)


def embed_kernel(scale, mm, tab, charges, blocks_in, count_in, atoms_in, slots_in, *rest):
    pieces, (out, c8, left, total, blocks, count, atoms, slots, sems) = rest[:-9], rest[-9:]
    begins = [sum(piece.shape[1] for piece in pieces[:i]) for i in range(len(pieces))]
    copies = fetch(
        (atoms_in, slots_in, blocks_in, count_in) + pieces,
        [atoms, slots, blocks, count]
        + [out.at[:, pl.ds(begin, piece.shape[1])] for begin, piece in zip(begins, pieces)],
        sems,
    )
    turned = tab[:, :LANES].T
    charge = charges[...].T[:ML_DEV]
    c8[...] = jnp.zeros_like(c8)
    c8[pl.ds(0, ML_DEV, stride=8), :] = charge
    for c in range(3):
        c8[pl.ds(c + 1, ML_DEV, stride=8), :] = charge * turned[ML_DEV * c : ML_DEV * (c + 1)]

    def charge_tile(t, carry):
        one, two, _ = three_parts(c8[pl.ds(pl.multiple_of(t * 8, 8), 8), :])
        left[:, pl.ds(pl.multiple_of(t * LANES, LANES), LANES)] = jnp.concatenate([one, two], axis=0).astype(
            jnp.bfloat16
        )
        return carry

    lax.fori_loop(0, ML_DEV, charge_tile, 0)
    nslots = blocks.shape[1]
    total[...] = jnp.zeros_like(total)
    copies[0].wait()
    copies[1].wait()

    def tile(i, carry):
        cols = pl.ds(pl.multiple_of(i * 256, 256), 256)
        some = atoms[:, cols]
        lhs = left[:, cols]
        for s in range(nslots // 2):
            inv = lax.rsqrt(rows0(some, slots[:, s * 256 : (s + 1) * 256]))
            cube = inv * inv * inv
            high = cube.astype(jnp.bfloat16)
            low = (cube - high.astype(jnp.float32)).astype(jnp.bfloat16)
            total[:, s * 256 : (s + 1) * 256] += jnp.dot(lhs, high, preferred_element_type=jnp.float32) + jnp.dot(
                lhs, low, preferred_element_type=jnp.float32
            )
        return carry

    lax.fori_loop(0, ML_DEV // 2, tile, 0, unroll=20)
    for copy in copies[2:]:
        copy.wait()
    for s in range(nslots):
        here = pl.ds(pl.multiple_of(blocks[0, s] * LANES, LANES), LANES)
        rows = mm[:, here]
        q = rows[3:4] * (scale * jnp.where(s < count[0], 1.0, 0.0))
        sums = total[:, s * LANES : (s + 1) * LANES]
        sums = sums[:8] + sums[8:]
        out[:, here] += q * (rows[:3] * sums[0:1] - sums[1:4])


def embed(blocks, count, mm, tab, charges, atoms, slots, pieces, scale):
    vmem = pl.BlockSpec(memory_space=pltpu.VMEM)
    return pl.pallas_call(
        functools.partial(embed_kernel, scale),
        out_shape=jax.ShapeDtypeStruct((3, mm.shape[1]), jnp.float32),
        in_specs=[vmem] * 3 + [pl.BlockSpec(memory_space=pltpu.HBM)] * (4 + len(pieces)),
        out_specs=vmem,
        scratch_shapes=[
            pltpu.VMEM((8 * ML_DEV, LANES), jnp.float32),
            pltpu.VMEM((16, ML_DEV * LANES), jnp.bfloat16),
            pltpu.VMEM((16, slots.shape[1]), jnp.float32),
            pltpu.SMEM(blocks.shape, blocks.dtype),
            pltpu.SMEM(count.shape, count.dtype),
            pltpu.VMEM(atoms.shape, atoms.dtype),
            pltpu.VMEM(slots.shape, slots.dtype),
            pltpu.SemaphoreType.DMA((4 + len(pieces),)),
        ],
        compiler_params=vmem_mib(28),
        name="embed_forces",
    )(mm, tab, charges, blocks, count, atoms, slots, *pieces)


def stage_parts(value, stage):
    parts = [value]
    for k in range(1, 4):
        pairs = []
        for dev in range(NDEV):
            at = [dev >> 5, 2 * ((dev >> 4) & 1) + ((dev >> 1) & 1), (dev >> 2) & 3]
            axis = STAGES[dev & 1][stage]
            at[axis] = (at[axis] + k) % 4
            x, y, z = at
            pairs.append((dev, (x << 5) + ((y >> 1) << 4) + (z << 2) + ((y & 1) << 1) + (dev & 1)))
        parts.append(lax.ppermute(value, ALL, pairs))
    return parts


def ring_parts(value, axis):
    n = lax.axis_size(axis)
    return [value] + [lax.ppermute(value, axis, [(i, (i + k) % n) for i in range(n)]) for k in range(1, n)]


def stand(value, zero):
    return value + zero[:, : value.shape[1]].astype(value.dtype)


def body(
    mm_atoms,
    neighbours,
    embed_blocks,
    embed_count,
    ml_coords,
    ml_species,
    ml_edges,
    species_table,
    field_weight,
    msg_weight,
    radial_weight,
    mix_weight,
    charge_weight,
    energy_weight,
):
    own_rows = mm_atoms.shape[1]
    kappa = 4.0 / math.sqrt(NDEV * ML_DEV)
    kappa_field = 3.0 / math.sqrt(NDEV * embed_blocks.shape[1] * LANES)
    me = lax.axis_index(ALL)[None]
    tab = lax.all_to_all(spread(ml_coords, ml_species[None]), ALL, 0, 0, tiled=True)
    tab = tab.reshape(NDEV, 2 * LANES)
    ids = ml_edges.reshape(-1, 1)
    blocks = own_rows // LANES
    cuts = (0, 12, 44, 52, 68, 100, blocks - 12, blocks)
    far = ml_coords

    def pairs(i, *after, before=far, behind=far):
        return pair_forces(cuts[i], cuts[i + 1] - cuts[i], before, mm_atoms, behind, neighbours, after)

    pieces = [None] * (len(cuts) - 1)
    pieces[1], zero = pairs(1, embed_blocks, radial_weight)
    pot, atoms, slots = field(embed_blocks, embed_count, mm_atoms, tab, pieces[1], kappa_field)
    basis, kinds, rows, zero = geometry(
        me, ids, tab, field_weight[None], charge_weight[None], energy_weight[None], pot
    )
    pot = functools.reduce(jnp.add, ring_parts(pot, "c"))
    pot = stand(functools.reduce(jnp.add, stage_parts(pot, 0)), zero)
    pot = functools.reduce(jnp.add, stage_parts(pot, 1))
    pot = functools.reduce(jnp.add, stage_parts(pot, 2))
    feat1, proj = first_layer(
        me, ids, pot, basis, kinds, species_table, rows, msg_weight, radial_weight, mix_weight
    )
    for i, stage in ((2, 0), (3, 1)):
        pieces[i], zero = pairs(i, proj)
        proj = stand(jnp.concatenate(stage_parts(proj, stage), axis=0), zero)
    halo = HALO_BLOCKS * LANES
    up = [(i, (i + 1) % NDEV) for i in range(NDEV)]
    down = [(j, i) for i, j in up]
    before = lax.ppermute(stand(mm_atoms[:, own_rows - halo :], zero), ALL, up)
    behind = lax.ppermute(stand(mm_atoms[:, :halo], zero), ALL, down)
    pieces[4], zero = pairs(4, proj)
    parts = stage_parts(proj, 2)
    parts[1:] = [stand(part, zero) for part in parts[1:]]
    parts = parts + [ring_parts(part, "c")[1] for part in parts]
    charges, energy = second_layer(
        me,
        ids,
        basis,
        feat1,
        radial_weight,
        mix_weight,
        rows,
        *parts,
    )
    pieces[5], _ = pairs(5, charges)
    for i in (0, 6):
        pieces[i], _ = pairs(i, charges, before=before, behind=behind)
    charges = lax.all_to_all(charges, ALL, 0, 0, tiled=True)
    mm_force = embed(embed_blocks, embed_count, mm_atoms, tab, charges, atoms, slots, pieces, kappa)
    return (energy[0, :ML_DEV], mm_force)


def solution(mesh):
    fine = Mesh(mesh.devices.reshape(4, 2, 4, 2, 2), ALL)
    in_specs = (
        P(None, ALL),
        P(None, ALL),
        P(ALL, None),
        P(ALL),
        P(None, ALL),
        P(ALL),
        P(ALL, None),
        P(),
        P(),
        P(),
        P(),
        P(),
        P(),
        P(),
    )
    out_specs = (P(ALL), P(None, ALL))
    return jax.shard_map(body, mesh=fine, in_specs=in_specs, out_specs=out_specs, check_vma=False)
```
